32 devices in a mesh: group: 2 (over x), dp: 2 (over y), tensor: 8 (over z, core).
Axes of the slice: x: 2, y: 2, z: 4, core: 2. Of those that a mesh axis runs over, the one named last changes fastest.
Arguments:
- image_feats: bfloat16 [512, 7680], P('tensor', ('group', 'dp')), may hold values from -6 to 6
- proj_weight: bfloat16 [7680, 8192], P(('group', 'dp'), 'tensor'), may hold values from -0.0625 to 0.0625
- proj_bias: bfloat16 [8192], P('tensor'), may hold values from -3 to 3
- kv_weight: bfloat16 [8192, 2048], P('tensor'), may hold values from -0.0625 to 0.0625
- queries: bfloat16 [1024, 8192], P(('group', 'dp'), 'tensor'), may hold values from -14 to 14
- out_grad: bfloat16 [1024, 8192], P(('group', 'dp'), 'tensor'), may hold values from -6 to 6
- image_sample: int32 [4, 128], P(('group', 'dp')), may hold values from 0 to 3, as said below
- text_sample: int32 [4, 256], P(('group', 'dp')), may hold values from 0 to 3, as said below
Outputs:
- attended: bfloat16 [1024, 8192], P(('group', 'dp'), 'tensor')
- d_queries: bfloat16 [1024, 8192], P(('group', 'dp'), 'tensor')
- d_proj_weight: bfloat16 [7680, 8192], P(('group', 'dp'), 'tensor')
- d_proj_bias: float32 [8192], P('tensor')
- d_kv_weight: bfloat16 [8192, 2048], P('tensor', ('group', 'dp'))
The draws below stay inside these ranges and needn't reach their ends.
Inputs may be any that keep to these rules, and one draw needn't show every extreme that they name: `image_sample`: within each row (one data shard) the sample numbers never fall and every number from 0 to 3 occurs. `text_sample`: within each row (one data shard) the sample numbers never fall and every number from 0 to 3 occurs.
All inputs are finite; a program needn't handle non-finite values.
Results may differ from the reference program's by a relative error of at most 0.04.
Values may be sent and summed in bfloat16 or wider, within the bound.
No kernel may reach another device: no remote copies, remote signals or barrier semaphores. Data moves between devices by JAX's collectives and lax.ppermute only.
A program may use at most 64 MiB of HBM per device.

```python
import jax
import jax.numpy as jnp
from jax import lax

VD = 7680
D = 8192
H = 64
KVH = 8
HD = 128
IMG_DEV = 128
TXT_DEV = 256
SAMPLES = 4
DATA = 4
IMAGE_ROWS = 512
TEXT_ROWS = 1024
KV_COLS = 2048


def sample_numbers(key, length):
    jitter = max(1, length // (2 * SAMPLES))
    base = jnp.arange(1, SAMPLES, dtype=jnp.int32) * length // SAMPLES
    offsets = jax.random.randint(key, (DATA, SAMPLES - 1), 0, jitter + 1, dtype=jnp.int32)
    cuts = base[None, :] + offsets
    places = jnp.arange(length, dtype=jnp.int32)
    return jnp.sum((places[None, :, None] >= cuts[:, None, :]).astype(jnp.int32), axis=2)


def draw_image_sample(key, part):
    return sample_numbers(jax.random.fold_in(key, 11), IMG_DEV)


def draw_text_sample(key, part):
    return sample_numbers(jax.random.fold_in(key, 12), TXT_DEV)


def draw_queries(key, part):
    first = jax.random.fold_in(jax.random.fold_in(key, 13), 0)
    shape = (TEXT_ROWS, H * HD)
    values = jnp.clip(jax.random.normal(first, shape, jnp.float32), -6.0, 6.0)
    return values.astype(jnp.bfloat16)


def strengthened(values, own_key, source, target, blocks, factor):
    owner, partner = [(jnp.arange(values.shape[axis_at]) // (values.shape[axis_at] // blocks)).reshape([-1 if axis == axis_at else 1 for axis in range(values.ndim)]) for axis_at in (source, target)]
    chosen = jax.random.permutation(own_key, blocks)[partner]
    strong = (owner == chosen) | (owner == (partner + blocks // 2) % blocks)
    return jnp.where(strong, factor * values, values)


def level_of(rng, dims, cuts, smallest, top_value):
    gain, own = 1.0, jax.random.fold_in(rng, 6)
    for axis_at, parts in cuts:
        heights = jnp.exp(jax.random.uniform(jax.random.fold_in(own, axis_at), (parts,), jnp.float32, smallest / len(cuts), top_value / len(cuts)))
        gain = gain * jnp.repeat(heights, dims[axis_at] // parts).reshape([-1 if axis == axis_at else 1 for axis in range(len(dims))])
    return gain


def bell_draw(own_key, dims, width, limit, cuts=(), held_as=jnp.bfloat16):
    gain = level_of(own_key, dims, cuts, -0.22, 0.18) if cuts else 1.0
    values = jax.random.normal(own_key, dims, jnp.float32) * width * gain
    return jnp.minimum(jnp.maximum(values, -limit), limit).astype(held_as)


def gaussian_with(key, extent, scale, most, cuts, heavy, kind=jnp.bfloat16):
    values = scale * jax.random.normal(key, extent, jnp.float32)
    if cuts:
        values = values * level_of(key, extent, cuts, -0.22, 0.18)
    return jnp.clip(strengthened(values, jax.random.fold_in(key, 3), *heavy), -most, most).astype(kind)


def setup_inputs(seed: int = 0) -> dict:
    streams_of = jax.random.split(jax.random.key(seed), 9)
    return {
        "image_feats": gaussian_with(streams_of[0], (IMAGE_ROWS, VD), 1.0, 6.0, ((0, 8), (1, 4)), (1, 0, 8, 2.0)),
        "proj_weight": bell_draw(streams_of[1], (VD, D), VD ** -0.5, 0.0625, ((0, 4), (1, 8))),
        "proj_bias": bell_draw(streams_of[2], (D,), 0.5, 3.0, ((0, 8),)),
        "kv_weight": bell_draw(streams_of[3], (D, KV_COLS), D ** -0.5, 0.0625, ((0, 8),)),
        "queries": draw_queries(jax.random.fold_in(streams_of[8], 71), 0),
        "out_grad": bell_draw(streams_of[5], (TEXT_ROWS, H * HD), 1.0, 6.0, ((0, 4), (1, 8))),
        "image_sample": draw_image_sample(jax.random.fold_in(streams_of[8], 71), 0),
        "text_sample": draw_text_sample(jax.random.fold_in(streams_of[8], 71), 0),
    }


def shard_attention(q_rows, keys, values, grads, image_ids, text_ids):
    scale = HD ** -0.5
    qf = q_rows.astype(jnp.float32)
    kf = keys.astype(jnp.float32)
    vf = values.astype(jnp.float32)
    gf = grads.astype(jnp.float32)
    scores = jnp.einsum('thd,ihd->hti', qf, kf) * scale
    allowed = text_ids[:, None] == image_ids[None, :]
    scores = jnp.where(allowed[None], scores, jnp.float32(-1e30))
    peak = jnp.max(scores, axis=-1, keepdims=True)
    expo = jnp.exp(scores - peak)
    probs = expo / jnp.sum(expo, axis=-1, keepdims=True)
    probs_b = probs.astype(jnp.bfloat16)
    pf = probs_b.astype(jnp.float32)
    attended = jnp.einsum('hti,ihd->thd', pf, vf).astype(jnp.bfloat16)
    dprobs = jnp.einsum('thd,ihd->hti', gf, vf)
    delta = jnp.sum(probs * dprobs, axis=-1, keepdims=True)
    dscores = (probs * (dprobs - delta) * scale).astype(jnp.bfloat16)
    df = dscores.astype(jnp.float32)
    d_rows = jnp.einsum('hti,ihd->thd', df, kf).astype(jnp.bfloat16)
    d_keys = jnp.einsum('hti,thd->ihd', df, qf)
    d_values = jnp.einsum('hti,thd->ihd', pf, gf)
    return attended, d_rows, d_keys, d_values


def reference(image_feats, proj_weight, proj_bias, kv_weight, queries, out_grad, image_sample, text_sample):
    block = VD // DATA

    def add_block(total, index):
        feats = lax.dynamic_slice_in_dim(image_feats, index * block, block, 1)
        weight = lax.dynamic_slice_in_dim(proj_weight, index * block, block, 0)
        part = jnp.dot(feats, weight, preferred_element_type=jnp.float32).astype(jnp.bfloat16)
        return total + part.astype(jnp.float32), None

    summed, _ = lax.scan(add_block, jnp.zeros((IMAGE_ROWS, D), jnp.float32), jnp.arange(DATA, dtype=jnp.int32))
    projected = (summed + proj_bias.astype(jnp.float32)[None, :]).astype(jnp.bfloat16)
    kv = jnp.dot(projected, kv_weight, preferred_element_type=jnp.float32).astype(jnp.bfloat16)
    half = KVH * HD
    shared = H // KVH
    keys = jnp.repeat(kv[:, :half].reshape(DATA, IMG_DEV, KVH, HD), shared, axis=2)
    values = jnp.repeat(kv[:, half:].reshape(DATA, IMG_DEV, KVH, HD), shared, axis=2)
    q_rows = queries.reshape(DATA, TXT_DEV, H, HD)
    grads = out_grad.reshape(DATA, TXT_DEV, H, HD)

    def one_shard(items):
        return shard_attention(*items)

    attended, d_rows, d_keys, d_values = lax.map(one_shard, (q_rows, keys, values, grads, image_sample, text_sample))
    d_keys = jnp.sum(d_keys.reshape(DATA, IMG_DEV, KVH, shared, HD), axis=3).reshape(IMAGE_ROWS, half)
    d_values = jnp.sum(d_values.reshape(DATA, IMG_DEV, KVH, shared, HD), axis=3).reshape(IMAGE_ROWS, half)
    dkv = jnp.concatenate([d_keys, d_values], axis=1).astype(jnp.bfloat16)
    d_projected = jnp.dot(dkv, kv_weight.T, preferred_element_type=jnp.float32).astype(jnp.bfloat16)

    def add_shard(total, index):
        rows = lax.dynamic_slice_in_dim(projected, index * IMG_DEV, IMG_DEV, 0)
        grads_rows = lax.dynamic_slice_in_dim(dkv, index * IMG_DEV, IMG_DEV, 0)
        part = jnp.dot(rows.T, grads_rows, preferred_element_type=jnp.float32).astype(jnp.bfloat16)
        return total + part.astype(jnp.float32), None

    kv_total, _ = lax.scan(add_shard, jnp.zeros((D, KV_COLS), jnp.float32), jnp.arange(DATA, dtype=jnp.int32))
    d_kv_weight = kv_total.astype(jnp.bfloat16)
    d_proj_weight = jnp.dot(image_feats.T, d_projected, preferred_element_type=jnp.float32).astype(jnp.bfloat16)
    d_proj_bias = jnp.sum(d_projected.astype(jnp.float32), axis=0)
    attended = attended.reshape(TEXT_ROWS, H * HD)
    d_queries = d_rows.reshape(TEXT_ROWS, H * HD)
    return attended, d_queries, d_proj_weight, d_proj_bias, d_kv_weight
```

```python
import jax
import jax.numpy as jnp
from jax import lax
from jax.sharding import PartitionSpec as P

HD = 128

T = "tensor"
XY = ("group", "dp")
F32 = jnp.float32
BF16 = jnp.bfloat16


def size_of(axes):
    names = axes if isinstance(axes, tuple) else (axes,)
    total = 1
    for name in names:
        total *= lax.axis_size(name)
    return total


def swap(x, axes, bits):
    return lax.ppermute(x, axes, [(i, i ^ bits) for i in range(size_of(axes))])


def send(x, axes, target):
    pairs = [(i, target(i)) for i in range(size_of(axes))]
    return lax.ppermute(x, axes, [(i, t) for i, t in pairs if t is not None])


def gather_line(block, chips):
    if chips != 4:
        return [block] + [swap(block, T, 2 * k) for k in range(1, chips)]
    chip = lax.axis_index(T) // 2
    inner = jnp.logical_or(chip == 1, chip == 2)
    near = swap(block, T, 2)
    middle = send(block, T, lambda i: i ^ 6 if i // 2 in (1, 2) else None)
    onward = jnp.where(inner, middle, block)
    cycle = {0: 2, 2: 3, 3: 1, 1: 0}
    two = send(onward, T, lambda i: 2 * cycle[i // 2] + i % 2)
    out = {1: 0, 2: 3}
    last = send(two, T, lambda i: 2 * out[i // 2] + i % 2 if i // 2 in out else None)
    return [block, near, two, jnp.where(inner, middle, last)]


def heads_per_key(queries, kv_weight):
    heads = queries.shape[1] // HD * lax.axis_size(T)
    return heads // (kv_weight.shape[1] // 2 // HD)


def from_partner(shard, axis, distance):
    return lax.ppermute(shard, axis, [(i, i ^ 1 << distance) for i in range(lax.axis_size(axis))])


def general(
    image_feats, proj_weight, proj_bias, kv_weight, queries, out_grad, image_sample, text_sample
):
    gathered = lax.all_gather(image_feats, "tensor", axis=0, tiled=True)
    rows = gathered
    summed = lax.psum_scatter(
        jnp.dot(rows, proj_weight, preferred_element_type=jnp.float32).astype(jnp.bfloat16),
        ("group", "dp"),
        scatter_dimension=0,
        tiled=True,
    ).astype(jnp.float32)
    projected = (summed + proj_bias.astype(jnp.float32)[None, :]).astype(jnp.bfloat16)
    kv_term = jnp.dot(projected, kv_weight, preferred_element_type=jnp.float32)
    kv_all = lax.psum(kv_term, "tensor").astype(jnp.bfloat16)
    local_heads = queries.shape[1] // HD
    shared = heads_per_key(queries, kv_weight)
    half = kv_all.shape[1] // 2
    key_head = lax.axis_index("tensor") * local_heads // shared
    key_start = key_head * HD
    keys = lax.dynamic_slice_in_dim(kv_all, key_start, HD, 1)
    values = lax.dynamic_slice_in_dim(kv_all, key_start + half, HD, 1)
    scale = HD ** (-0.5)
    q_rows = queries.reshape(queries.shape[0], local_heads, HD)
    grads = out_grad.reshape(out_grad.shape[0], local_heads, HD)
    scores = jnp.einsum("thd,id->hti", q_rows, keys, preferred_element_type=jnp.float32) * scale
    allowed = text_sample[0][:, None] == image_sample[0][None, :]
    scores = jnp.where(allowed[None], scores, jnp.float32(-1e30))
    peak = jnp.max(scores, axis=-1, keepdims=True)
    expo = jnp.exp(scores - peak)
    probs = expo / jnp.sum(expo, axis=-1, keepdims=True)
    probs_b = probs.astype(jnp.bfloat16)
    attended = jnp.einsum(
        "hti,id->thd", probs_b, values, preferred_element_type=jnp.float32
    ).astype(jnp.bfloat16)
    dprobs = jnp.einsum("thd,id->hti", grads, values, preferred_element_type=jnp.float32)
    delta = jnp.sum(probs * dprobs, axis=-1, keepdims=True)
    dscores = (probs * (dprobs - delta) * scale).astype(jnp.bfloat16)
    d_rows = jnp.einsum("hti,id->thd", dscores, keys, preferred_element_type=jnp.float32).astype(
        jnp.bfloat16
    )
    d_keys = jnp.einsum("hti,thd->id", dscores, q_rows, preferred_element_type=jnp.float32)
    d_values = jnp.einsum("hti,thd->id", probs_b, grads, preferred_element_type=jnp.float32)
    image_count = kv_term.shape[0]
    members = shared // local_heads
    stacked = jnp.concatenate([d_keys, d_values], axis=1)
    for level in range(members.bit_length() - 1):
        stacked = stacked + from_partner(stacked, "tensor", level)
    width = stacked.shape[1] // members
    member = lax.axis_index("tensor") % members
    mine = lax.dynamic_slice_in_dim(stacked, member * width, width, 1).astype(jnp.bfloat16)
    collected = lax.all_gather(mine, "tensor", axis=1, tiled=True)
    heads_total = collected.shape[1] // (2 * HD)
    dkv = (
        collected.reshape(image_count, heads_total, 2, HD)
        .transpose(0, 2, 1, 3)
        .reshape(image_count, 2 * heads_total * HD)
    )
    d_projected = lax.dot_general(
        dkv, kv_weight, (((1,), (1,)), ((), ())), preferred_element_type=jnp.float32
    ).astype(jnp.bfloat16)
    kv_grad_term = lax.dot_general(
        projected, dkv, (((0,), (0,)), ((), ())), preferred_element_type=jnp.float32
    )
    d_kv_weight = lax.psum_scatter(
        kv_grad_term.astype(jnp.bfloat16), ("group", "dp"), scatter_dimension=1, tiled=True
    )
    piece = lax.all_gather(d_projected, ("group", "dp"), axis=0, tiled=True)
    rows = gathered
    weight_grad = lax.dot_general(
        rows, piece, (((0,), (0,)), ((), ())), preferred_element_type=jnp.float32
    )
    bias_grad = jnp.sum(piece.astype(jnp.float32), axis=0)
    weight_grad, bias_grad = (weight_grad, bias_grad)
    attended = attended.reshape(queries.shape)
    d_queries = d_rows.reshape(queries.shape)
    return (attended, d_queries, weight_grad.astype(jnp.bfloat16), bias_grad, d_kv_weight)


def shards(
    image_feats, proj_weight, proj_bias, kv_weight, queries, out_grad, image_sample, text_sample
):
    chips = lax.axis_size(T) // 2
    parts = size_of(XY)
    if heads_per_key(queries, kv_weight) * HD != queries.shape[1] or chips != parts:
        return general(
            image_feats, proj_weight, proj_bias, kv_weight, queries, out_grad, image_sample, text_sample
        )
    me = lax.axis_index(T)
    chip, core = me // 2, me % 2
    part = lax.axis_index("group") * lax.axis_size("dp") + lax.axis_index("dp")

    def pick(stack, k):
        return lax.dynamic_index_in_dim(stack, k, 0, keepdims=False)

    def both_cores(own, other, axis):
        return jnp.where(core == 0, jnp.stack([own, other], axis), jnp.stack([other, own], axis))

    own = jnp.stack(gather_line(image_feats, chips))
    other = swap(own, T, 1)
    feats = both_cores(own, other, 1)
    shard_rows = 2 * image_feats.shape[0]
    feats = feats.reshape(chips, shard_rows, image_feats.shape[1])
    partial = jnp.einsum("krf,fd->krd", feats, proj_weight, preferred_element_type=F32).astype(BF16)
    summed = pick(partial, chip ^ part).astype(F32)
    for j in range(1, parts):
        summed = summed + swap(pick(partial, chip ^ part ^ j), XY, j).astype(F32)
    projected = (summed + proj_bias.astype(F32)[None, :]).astype(BF16)
    projected_all = jnp.stack([projected] + [swap(projected, XY, j) for j in range(1, parts)])

    kv_term = jnp.dot(projected, kv_weight, preferred_element_type=F32)
    half = kv_weight.shape[1] // 2
    tensors = 2 * chips

    def kv_of(i):
        start = (me ^ i) * HD
        return jnp.concatenate(
            [
                lax.dynamic_slice_in_dim(kv_term, start, HD, 1),
                lax.dynamic_slice_in_dim(kv_term, half + start, HD, 1),
            ],
            axis=1,
        )

    theirs = swap(jnp.stack([kv_of(2 * k + 1) for k in range(chips)]).astype(BF16), T, 1)
    mine = jnp.stack([kv_of(2 * k) for k in range(chips)]) + theirs.astype(F32)
    kv = mine[0]
    for k in range(1, chips):
        kv = kv + swap(mine[k].astype(BF16), T, 2 * k).astype(F32)
    kv = kv.astype(BF16)
    keys, values = kv[:, :HD], kv[:, HD:]

    local_heads = queries.shape[1] // HD
    scale = HD ** (-0.5)
    q_rows = queries.reshape(queries.shape[0], local_heads, HD)
    grads = out_grad.reshape(out_grad.shape[0], local_heads, HD)
    scores = jnp.einsum("thd,id->hti", q_rows, keys, preferred_element_type=F32) * scale
    allowed = text_sample[0][:, None] == image_sample[0][None, :]
    scores = jnp.where(allowed[None], scores, F32(-1e30))
    peak = jnp.max(scores, axis=-1, keepdims=True)
    expo = jnp.exp(scores - peak)
    probs = expo / jnp.sum(expo, axis=-1, keepdims=True)
    probs_b = probs.astype(BF16)
    attended = jnp.einsum("hti,id->thd", probs_b, values, preferred_element_type=F32).astype(BF16)
    dprobs = jnp.einsum("thd,id->hti", grads, values, preferred_element_type=F32)
    delta = jnp.sum(probs * dprobs, axis=-1, keepdims=True)
    dscores = (probs * (dprobs - delta) * scale).astype(BF16)
    d_rows = jnp.einsum("hti,id->thd", dscores, keys, preferred_element_type=F32).astype(BF16)
    d_keys = jnp.einsum("hti,thd->id", dscores, q_rows, preferred_element_type=F32)
    d_values = jnp.einsum("hti,thd->id", probs_b, grads, preferred_element_type=F32)
    dkv = jnp.concatenate([d_keys, d_values], axis=1).astype(BF16)

    dkv_own = jnp.stack([dkv] + [swap(dkv, T, 2 * k) for k in range(1, chips)])
    dkv_other = swap(dkv_own, T, 1)
    heads = both_cores(dkv_own, dkv_other, 1)
    heads = jnp.stack([pick(heads, k ^ chip) for k in range(chips)])
    rows = heads.shape[2]
    dkv_all = heads.reshape(tensors, rows, 2, HD).transpose(1, 2, 0, 3).reshape(rows, 2 * tensors * HD)
    d_projected = lax.dot_general(
        dkv_all, kv_weight, (((1,), (1,)), ((), ())), preferred_element_type=F32
    ).astype(BF16)
    width = kv_weight.shape[1] // parts

    def columns(j):
        return lax.dynamic_slice_in_dim(dkv_all, (part ^ j) * width, width, 1)

    dkv_rows = jnp.stack([columns(0)] + [swap(columns(j), XY, j) for j in range(1, parts)])
    d_kv_weight = jnp.einsum(
        "jrd,jrc->dc", projected_all, dkv_rows, preferred_element_type=F32
    ).astype(BF16)
    d_all = jnp.stack([d_projected] + [swap(d_projected, XY, j) for j in range(1, parts)])
    d_by_chip = jnp.stack([pick(d_all, k ^ chip ^ part) for k in range(parts)])
    weight_grad = jnp.einsum(
        "krf,krd->fd", feats, d_by_chip, preferred_element_type=F32
    ).astype(BF16)
    bias_grad = jnp.sum(d_all.astype(F32), axis=(0, 1))
    return (
        attended.reshape(queries.shape),
        d_rows.reshape(queries.shape),
        weight_grad,
        bias_grad,
        d_kv_weight,
    )


def solution(mesh):
    in_specs = (
        P("tensor", ("group", "dp")),
        P(("group", "dp"), "tensor"),
        P("tensor"),
        P("tensor", None),
        P(("group", "dp"), "tensor"),
        P(("group", "dp"), "tensor"),
        P(("group", "dp"), None),
        P(("group", "dp"), None),
    )
    out_specs = (
        P(("group", "dp"), "tensor"),
        P(("group", "dp"), "tensor"),
        P(("group", "dp"), "tensor"),
        P("tensor"),
        P("tensor", ("group", "dp")),
    )
    return jax.shard_map(shards, mesh=mesh, in_specs=in_specs, out_specs=out_specs, check_vma=False)
```

```python
import functools

import jax
import jax.numpy as jnp
from jax import lax
from jax.experimental import pallas as pl
from jax.experimental.pallas import tpu as pltpu
from jax.sharding import PartitionSpec as P

HD = 128

T = "tensor"
XY = ("group", "dp")
F32 = jnp.float32
BF16 = jnp.bfloat16
NT = (((1,), (1,)), ((), ()))
TN = (((0,), (0,)), ((), ()))
VMEM_LIMIT = 8 * 1024 * 1024


def size_of(axes):
    names = axes if isinstance(axes, tuple) else (axes,)
    total = 1
    for name in names:
        total *= lax.axis_size(name)
    return total


def swap(x, axes, bits):
    return lax.ppermute(x, axes, [(i, i ^ bits) for i in range(size_of(axes))])


def after(x, *others):
    return lax.optimization_barrier((x,) + others)[0]


def heads_per_key(queries, kv_weight):
    heads = queries.shape[1] // HD * lax.axis_size(T)
    return heads // (kv_weight.shape[1] // 2 // HD)


def from_partner(shard, axis, distance):
    return lax.ppermute(shard, axis, [(i, i ^ 1 << distance) for i in range(lax.axis_size(axis))])


def general(
    image_feats, proj_weight, proj_bias, kv_weight, queries, out_grad, image_sample, text_sample
):
    gathered = lax.all_gather(image_feats, "tensor", axis=0, tiled=True)
    rows = gathered
    summed = lax.psum_scatter(
        jnp.dot(rows, proj_weight, preferred_element_type=jnp.float32).astype(jnp.bfloat16),
        ("group", "dp"),
        scatter_dimension=0,
        tiled=True,
    ).astype(jnp.float32)
    projected = (summed + proj_bias.astype(jnp.float32)[None, :]).astype(jnp.bfloat16)
    kv_term = jnp.dot(projected, kv_weight, preferred_element_type=jnp.float32)
    kv_all = lax.psum(kv_term, "tensor").astype(jnp.bfloat16)
    local_heads = queries.shape[1] // HD
    shared = heads_per_key(queries, kv_weight)
    half = kv_all.shape[1] // 2
    key_head = lax.axis_index("tensor") * local_heads // shared
    key_start = key_head * HD
    keys = lax.dynamic_slice_in_dim(kv_all, key_start, HD, 1)
    values = lax.dynamic_slice_in_dim(kv_all, key_start + half, HD, 1)
    scale = HD ** (-0.5)
    q_rows = queries.reshape(queries.shape[0], local_heads, HD)
    grads = out_grad.reshape(out_grad.shape[0], local_heads, HD)
    scores = jnp.einsum("thd,id->hti", q_rows, keys, preferred_element_type=jnp.float32) * scale
    allowed = text_sample[0][:, None] == image_sample[0][None, :]
    scores = jnp.where(allowed[None], scores, jnp.float32(-1e30))
    peak = jnp.max(scores, axis=-1, keepdims=True)
    expo = jnp.exp(scores - peak)
    probs = expo / jnp.sum(expo, axis=-1, keepdims=True)
    probs_b = probs.astype(jnp.bfloat16)
    attended = jnp.einsum(
        "hti,id->thd", probs_b, values, preferred_element_type=jnp.float32
    ).astype(jnp.bfloat16)
    dprobs = jnp.einsum("thd,id->hti", grads, values, preferred_element_type=jnp.float32)
    delta = jnp.sum(probs * dprobs, axis=-1, keepdims=True)
    dscores = (probs * (dprobs - delta) * scale).astype(jnp.bfloat16)
    d_rows = jnp.einsum("hti,id->thd", dscores, keys, preferred_element_type=jnp.float32).astype(
        jnp.bfloat16
    )
    d_keys = jnp.einsum("hti,thd->id", dscores, q_rows, preferred_element_type=jnp.float32)
    d_values = jnp.einsum("hti,thd->id", probs_b, grads, preferred_element_type=jnp.float32)
    image_count = kv_term.shape[0]
    members = shared // local_heads
    stacked = jnp.concatenate([d_keys, d_values], axis=1)
    for level in range(members.bit_length() - 1):
        stacked = stacked + from_partner(stacked, "tensor", level)
    width = stacked.shape[1] // members
    member = lax.axis_index("tensor") % members
    mine = lax.dynamic_slice_in_dim(stacked, member * width, width, 1).astype(jnp.bfloat16)
    collected = lax.all_gather(mine, "tensor", axis=1, tiled=True)
    heads_total = collected.shape[1] // (2 * HD)
    dkv = (
        collected.reshape(image_count, heads_total, 2, HD)
        .transpose(0, 2, 1, 3)
        .reshape(image_count, 2 * heads_total * HD)
    )
    d_projected = lax.dot_general(
        dkv, kv_weight, (((1,), (1,)), ((), ())), preferred_element_type=jnp.float32
    ).astype(jnp.bfloat16)
    kv_grad_term = lax.dot_general(
        projected, dkv, (((0,), (0,)), ((), ())), preferred_element_type=jnp.float32
    )
    d_kv_weight = lax.psum_scatter(
        kv_grad_term.astype(jnp.bfloat16), ("group", "dp"), scatter_dimension=1, tiled=True
    )
    piece = lax.all_gather(d_projected, ("group", "dp"), axis=0, tiled=True)
    rows = gathered
    weight_grad = lax.dot_general(
        rows, piece, (((0,), (0,)), ((), ())), preferred_element_type=jnp.float32
    )
    bias_grad = jnp.sum(piece.astype(jnp.float32), axis=0)
    weight_grad, bias_grad = (weight_grad, bias_grad)
    attended = attended.reshape(queries.shape)
    d_queries = d_rows.reshape(queries.shape)
    return (attended, d_queries, weight_grad.astype(jnp.bfloat16), bias_grad, d_kv_weight)


def params():
    return pltpu.CompilerParams(vmem_limit_bytes=VMEM_LIMIT)


def cost(flops, nbytes):
    return pl.CostEstimate(flops=flops, bytes_accessed=nbytes, transcendentals=0)


def whole(shape):
    return pl.BlockSpec(shape, lambda *_: (0,) * len(shape))


def place_of():
    me = lax.axis_index(T)
    part = lax.axis_index("group") * lax.axis_size("dp") + lax.axis_index("dp")
    return (me // 2) ^ part, me % 2, me, part


def pack_kernel(*refs):
    out = refs[-1]
    width = out.shape[2]
    for i, ref in enumerate(refs[:-1]):
        out[i] = ref[:, ref.shape[1] - width :]


def pack(*arrays):
    rows, width = arrays[0].shape[0], min(x.shape[1] for x in arrays)
    return pl.pallas_call(
        pack_kernel,
        in_specs=in_vmem(len(arrays)),
        out_shape=jax.ShapeDtypeStruct((len(arrays), rows, width), BF16),
        compiler_params=params(),
        cost_estimate=cost(0, 8 * len(arrays) * rows * width),
        name="pack",
    )(*arrays)


def add_kernel(mine, theirs, first, *rest):
    first[...] = mine[0] + theirs[0].astype(F32)
    for k, ref in enumerate(rest):
        ref[...] = (mine[k + 1] + theirs[k + 1].astype(F32)).astype(BF16)


def add(mine, theirs):
    shape = mine.shape[1:]
    return pl.pallas_call(
        add_kernel,
        in_specs=in_vmem(2),
        out_shape=[jax.ShapeDtypeStruct(shape, F32)]
        + [jax.ShapeDtypeStruct(shape, BF16)] * (mine.shape[0] - 1),
        compiler_params=params(),
        cost_estimate=cost(0, 16 * mine.size),
        name="add",
    )(mine, theirs)


def tiles_of(width, tile):
    return width // tile if width % tile == 0 else 1


def project_kernel(groups, *refs):
    place = place_of()
    mine, others = refs[:groups], refs[groups : 2 * groups]
    weight, (partial, feats) = refs[2 * groups], (refs[2 * groups + 1 : -1], refs[-1])
    own = [ref.at[i] for ref in mine for i in range(ref.shape[0])]
    others = [ref.at[i] for ref in others for i in range(ref.shape[0])]
    count = len(own)
    rows = own[0].shape[0]
    for k in range(count):
        j = k ^ place[0]

        @pl.when(place[1] == 0)
        def _():
            feats[j, :rows, :] = own[k][...]
            feats[j, rows:, :] = others[k][...]

        @pl.when(place[1] != 0)
        def _():
            feats[j, :rows, :] = others[k][...]
            feats[j, rows:, :] = own[k][...]

    tiles = tiles_of(weight.shape[1], 256)
    tile = weight.shape[1] // tiles

    def step(n, _):
        at = pl.ds(pl.multiple_of(n * tile, tile), tile)
        lhs = feats[...].reshape(count * 2 * rows, feats.shape[2])
        out = jnp.dot(lhs, weight[:, at], preferred_element_type=F32).astype(BF16)
        for j in range(count):
            partial[j][:, at] = out[j * 2 * rows : (j + 1) * 2 * rows]
        return 0

    lax.fori_loop(0, tiles, step, 0)


def in_vmem(count):
    return [pl.BlockSpec()] * count


def project(own, others, weight):
    count = sum(x.shape[0] for x in own)
    rows, depth = own[0].shape[1:]
    width = weight.shape[1]
    return pl.pallas_call(
        functools.partial(project_kernel, len(own)),
        in_specs=in_vmem(2 * len(own) + 1),
        out_shape=[jax.ShapeDtypeStruct((2 * rows, width), BF16)] * count
        + [jax.ShapeDtypeStruct((count, 2 * rows, depth), BF16)],
        compiler_params=params(),
        cost_estimate=cost(8 * count * rows * depth * width, 2 * depth * width),
        name="project",
    )(*own, *others, weight)


def heads_into(x, place, odd, weight, out):
    half = weight.shape[1] // 2
    for i in range(out.shape[0]):
        start = pl.multiple_of((place[2] ^ (2 * i + odd)) * HD, HD)
        for at, cut in ((start, slice(0, HD)), (half + start, slice(HD, 2 * HD))):
            value = jnp.dot(x, weight[:, pl.ds(at, HD)], preferred_element_type=F32)
            out[i, :, cut] = value.astype(out.dtype)


def combine_kernel(parts, first, *refs):
    place = place_of()
    arrived, (bias, weight, projected, out) = refs[: parts - 1], refs[parts - 1 :]
    total = first[...].astype(F32)
    for ref in arrived:
        total = total + ref[...].astype(F32)
    x = (total + bias[...].astype(F32)).astype(BF16)
    projected[...] = x
    heads_into(x, place, 1, weight, out)


def combine(first, arrived, bias, kv_weight, tensors):
    parts = 1 + len(arrived)
    rows, depth = first.shape
    return pl.pallas_call(
        functools.partial(combine_kernel, parts),
        in_specs=in_vmem(parts + 2),
        out_shape=[
            jax.ShapeDtypeStruct((rows, depth), BF16),
            jax.ShapeDtypeStruct((tensors // 2, rows, 2 * HD), BF16),
        ],
        compiler_params=params(),
        cost_estimate=cost(24 * rows * depth * tensors * HD, depth * tensors * HD * 2),
        name="combine",
    )(first, *arrived, bias, kv_weight)


def own_heads_kernel(projected, weight, out):
    heads_into(projected[...], place_of(), 0, weight, out)


def own_heads(projected, kv_weight, tensors):
    rows, depth = projected.shape
    return pl.pallas_call(
        own_heads_kernel,
        in_specs=in_vmem(2),
        out_shape=jax.ShapeDtypeStruct((tensors // 2, rows, 2 * HD), F32),
        compiler_params=params(),
        cost_estimate=cost(24 * rows * depth * tensors * HD, depth * tensors * HD * 2),
        name="own_heads",
    )(projected, kv_weight)


def attend_kernel(count, *refs):
    first, arrived = refs[0], refs[1:count]
    queries, out_grad, image_ids, text_ids, kv_out, dkv, probs_out, dscores_out = refs[count:]
    total = first[...]
    for ref in arrived:
        total = total + ref[...].astype(F32)
    kv = total.astype(BF16)
    kv_out[...] = kv
    keys, values = kv[:, :HD], kv[:, HD:]
    scale = HD ** (-0.5)
    allowed = image_ids[...] == text_ids[...]
    d_keys = jnp.zeros((kv.shape[0], HD), F32)
    d_values = jnp.zeros((kv.shape[0], HD), F32)
    for head in range(queries.shape[1] // HD):
        at = slice(head * HD, (head + 1) * HD)
        q, g = queries[:, at], out_grad[:, at]
        scores = lax.dot_general(keys, q, NT, preferred_element_type=F32) * scale
        scores = jnp.where(allowed, scores, F32(-1e30))
        expo = jnp.exp(scores - jnp.max(scores, axis=0, keepdims=True))
        probs = expo * (1.0 / jnp.sum(expo, axis=0, keepdims=True))
        probs_b = probs.astype(BF16)
        dprobs = lax.dot_general(values, g, NT, preferred_element_type=F32)
        delta = jnp.sum(probs * dprobs, axis=0, keepdims=True)
        dscores = (probs * (dprobs - delta) * scale).astype(BF16)
        d_keys = d_keys + jnp.dot(dscores, q, preferred_element_type=F32)
        d_values = d_values + jnp.dot(probs_b, g, preferred_element_type=F32)
        probs_out[head] = probs_b
        dscores_out[head] = dscores
    dkv[:, :HD] = d_keys.astype(BF16)
    dkv[:, HD:] = d_values.astype(BF16)


def attend(first, arrived, queries, out_grad, image_ids, text_ids):
    inputs = [first, *arrived, queries, out_grad, image_ids, text_ids]
    shape = first.shape
    heads = queries.shape[1] // HD
    weights = jax.ShapeDtypeStruct((heads, shape[0], queries.shape[0]), BF16)
    return pl.pallas_call(
        functools.partial(attend_kernel, 1 + len(arrived)),
        out_shape=[
            jax.ShapeDtypeStruct(shape, BF16),
            jax.ShapeDtypeStruct(shape, BF16),
            weights,
            weights,
        ],
        compiler_params=params(),
        cost_estimate=cost(16 * 4 * queries.size * shape[0], 8 * queries.size),
        name="attend",
    )(*inputs)


def finish_kernel(kv, probs, dscores, attended, d_queries):
    keys, values = kv[:, :HD], kv[:, HD:]
    for head in range(probs.shape[0]):
        at = slice(head * HD, (head + 1) * HD)
        attended[:, at] = lax.dot_general(
            probs[head], values, TN, preferred_element_type=F32
        ).astype(BF16)
        d_queries[:, at] = lax.dot_general(
            dscores[head], keys, TN, preferred_element_type=F32
        ).astype(BF16)


def finish(kv, probs, dscores):
    heads, images, texts = probs.shape
    out = jax.ShapeDtypeStruct((texts, heads * HD), BF16)
    return pl.pallas_call(
        finish_kernel,
        out_shape=[out, out],
        compiler_params=params(),
        cost_estimate=cost(8 * 4 * heads * images * texts * HD, 8 * probs.size),
        name="finish",
    )(kv, probs, dscores)


def turn_kernel(feats, out):
    parts, rows, tile = feats.shape
    out[...] = feats[...].reshape(parts * rows, tile).T


def turn(feats):
    parts, rows, depth = feats.shape
    tile = depth // tiles_of(depth, 640)
    total = parts * rows
    return pl.pallas_call(
        turn_kernel,
        grid=(depth // tile,),
        in_specs=[pl.BlockSpec((parts, rows, tile), lambda n: (0, 0, n))],
        out_specs=pl.BlockSpec((tile, total), lambda n: (n, 0)),
        out_shape=jax.ShapeDtypeStruct((depth, total), BF16),
        compiler_params=params(),
        cost_estimate=cost(0, 8 * depth * total),
        name="turn",
    )(feats)


def back_columns(dkv, weight, first, targets):
    columns = targets[0].shape[1]
    count = tiles_of(columns, 256)
    tile = columns // count
    for n in range(count):
        value = lax.dot_general(
            dkv,
            weight[first + n * tile : first + (n + 1) * tile, :],
            NT,
            preferred_element_type=F32,
        ).astype(BF16)
        for ref in targets:
            ref[:, n * tile : (n + 1) * tile] = value


def back_kernel(chips, *refs):
    place = place_of()
    own, (other, weight, out), refs = refs[:chips], refs[chips : chips + 3], refs[chips + 3 :]
    sent, (cols, dkv_all) = refs[:-2], refs[-2:]
    columns = out.shape[1]
    half = dkv_all.shape[1] // 2
    for k in range(chips):
        for block, bits in ((own[k][...], 2 * k), (other[k], 2 * k + 1)):
            start = pl.multiple_of((place[2] ^ bits) * HD, HD)
            dkv_all[:, pl.ds(start, HD)] = block[:, :HD]
            dkv_all[:, pl.ds(half + start, HD)] = block[:, HD:]
    width = cols.shape[1] * 2
    for j in range(len(sent) + 1):
        for m in range(width // HD // 2):
            start = (place[3] ^ j) * width + (2 * m + place[1]) * HD
            block = dkv_all[:, pl.ds(pl.multiple_of(start, HD), HD)]
            at = slice(m * HD, (m + 1) * HD)
            if j == 0:
                cols[:, at] = block
            else:
                sent[j - 1][:, columns + m * HD : columns + (m + 1) * HD] = block
    back_columns(dkv_all[...], weight, 0, [out])
    for ref in sent:
        ref[:, :columns] = out[...]


def back(own, other, kv_weight, parts, chunks):
    rows = own[0].shape[0]
    depth, width = kv_weight.shape
    columns = depth // chunks
    extra = width // parts // 2
    full = jax.ShapeDtypeStruct((rows, columns + extra), BF16)
    return pl.pallas_call(
        functools.partial(back_kernel, len(own)),
        in_specs=in_vmem(len(own) + 2),
        out_shape=[jax.ShapeDtypeStruct((rows, columns), BF16)]
        + [full] * (parts - 1)
        + [
            jax.ShapeDtypeStruct((rows, extra), BF16),
            jax.ShapeDtypeStruct((rows, width), BF16),
        ],
        compiler_params=params(),
        cost_estimate=cost(8 * rows * columns * width, 2 * columns * width),
        name="back",
    )(*own, other, kv_weight)


def back_rest_kernel(chunk, dkv_all, weight, out):
    back_columns(dkv_all[...], weight, chunk * out.shape[1], [out])


def back_rest(dkv_all, kv_weight, chunk, chunks):
    rows = dkv_all.shape[0]
    depth, width = kv_weight.shape
    columns = depth // chunks
    return pl.pallas_call(
        functools.partial(back_rest_kernel, chunk),
        in_specs=in_vmem(2),
        out_shape=jax.ShapeDtypeStruct((rows, columns), BF16),
        compiler_params=params(),
        cost_estimate=cost(8 * rows * columns * width, 2 * columns * width),
        name="back_rest",
    )(dkv_all, kv_weight)


def kv_grad_kernel(count, parts, *refs):
    place = place_of()
    left, mine, (theirs, out, right) = refs[:count], refs[count : count + parts], refs[-3:]
    rows = left[0].shape[0]
    extra = mine[0].shape[1]
    for j in range(parts):
        at = slice(j * rows, (j + 1) * rows)
        skip = mine[j].shape[1] - extra
        for m in range(extra // HD):
            start = pl.multiple_of((2 * m + place[1]) * HD, HD)
            right[at, pl.ds(start, HD)] = mine[j][:, skip + m * HD : skip + (m + 1) * HD]
            start = pl.multiple_of((2 * m + 1 - place[1]) * HD, HD)
            right[at, pl.ds(start, HD)] = theirs[j, :, m * HD : (m + 1) * HD]
    depth = out.shape[0]
    count = tiles_of(depth, 256)
    tile = depth // count
    for n in range(count):
        at = slice(n * tile, (n + 1) * tile)
        lhs = jnp.concatenate([x[:, at] for x in left], axis=0)
        out[at, :] = lax.dot_general(
            lhs, right[...], TN, preferred_element_type=F32
        ).astype(BF16)


def kv_grad(left, own, sent, theirs):
    parts = 1 + len(sent)
    rows, depth = left[0].shape
    extra = own.shape[1]
    return pl.pallas_call(
        functools.partial(kv_grad_kernel, len(left), parts),
        in_specs=in_vmem(len(left) + parts + 1),
        out_shape=jax.ShapeDtypeStruct((depth, 2 * extra), BF16),
        scratch_shapes=[pltpu.VMEM((parts * rows, 2 * extra), BF16)],
        compiler_params=params(),
        cost_estimate=cost(4 * parts * rows * depth * extra, 4 * parts * rows * depth),
        name="kv_grad",
    )(*left, own, *sent, theirs)


def weight_grad_kernel(parts, feats, *refs):
    grads, (out, bias, right) = refs[:parts], refs[-3:]
    columns = out.shape[1]
    rows = grads[0].shape[0]

    @pl.when(pl.program_id(0) == 0)
    def _():
        total = None
        for j, g in enumerate(grads):
            value = g[:, :columns]
            right[j * rows : (j + 1) * rows, :] = value
            term = jnp.sum(value.astype(F32), axis=0, keepdims=True)
            total = term if total is None else total + term
        bias[...] = total

    tile = out.shape[0]
    at = pl.ds(pl.multiple_of(pl.program_id(0) * tile, tile), tile)
    out[...] = jnp.dot(feats[at, :], right[...], preferred_element_type=F32).astype(BF16)


def weight_grad(feats, grads, held, chunk, chunks):
    depth, total = feats.shape
    shard = grads[0].shape
    columns = shard[1]
    tile = depth // 3 if depth % 384 == 0 else depth
    inputs = [feats, *grads]
    specs = in_vmem(len(inputs))
    aliases = {}
    if held is not None:
        aliases = {len(inputs): 0, len(inputs) + 1: 1}
        inputs += held
        specs += [pl.BlockSpec(memory_space=pl.ANY)] * 2
    return pl.pallas_call(
        functools.partial(weight_grad_kernel, len(grads)),
        grid=(depth // tile,),
        in_specs=specs,
        out_specs=[
            pl.BlockSpec((tile, columns), lambda n: (n, chunk)),
            pl.BlockSpec((1, columns), lambda n: (0, chunk)),
        ],
        out_shape=[
            jax.ShapeDtypeStruct((depth, columns * chunks), BF16),
            jax.ShapeDtypeStruct((1, columns * chunks), F32),
        ],
        scratch_shapes=[pltpu.VMEM((total, columns), BF16)],
        input_output_aliases=aliases,
        compiler_params=params(),
        cost_estimate=cost(2 * total * depth * columns, 2 * depth * (total + columns)),
        name="weight_grad",
    )(*inputs)


def shards(
    image_feats, proj_weight, proj_bias, kv_weight, queries, out_grad, image_sample, text_sample
):
    tensors = lax.axis_size(T)
    chips = tensors // 2
    parts = size_of(XY)
    if (
        heads_per_key(queries, kv_weight) * HD != queries.shape[1]
        or chips != parts
        or parts != 4
    ):
        return general(
            image_feats, proj_weight, proj_bias, kv_weight, queries, out_grad, image_sample, text_sample
        )
    own = [image_feats] + [swap(image_feats, T, 2 * k) for k in range(1, chips)]
    image_ids = after(image_sample, own[1]).reshape(-1, 1)
    stacks = [pack(*own[: chips // 2]), pack(*own[chips // 2 :])]
    *partial, feats = project(stacks, [swap(x, T, 1) for x in stacks], proj_weight)
    arrived = [swap(partial[j], XY, j) for j in range(1, parts)]

    projected, theirs = combine(
        partial[0], arrived, proj_bias.reshape(1, -1), kv_weight, tensors
    )
    theirs = swap(theirs, T, 1)
    mine = own_heads(projected, kv_weight, tensors)
    mine, *kv_sent = add(mine, theirs)
    kv_parts = [swap(x, T, 2 * k) for k, x in enumerate(kv_sent, 1)]
    ready = after(projected, *kv_sent)
    aside, across = swap(ready, XY, 1), swap(ready, XY, 2)
    *kv_parts, aside, across = lax.optimization_barrier((*kv_parts, aside, across))

    kv, dkv, probs, dscores = attend(
        mine, kv_parts, queries, out_grad, image_ids, text_sample
    )
    cut = projected.shape[0] // 2
    upper, lower, _ = lax.optimization_barrier((across[:cut], aside[cut:], dkv))
    upper, lower = swap(upper, XY, 1), swap(lower, XY, 2)
    dkv_own = [dkv] + [swap(dkv, T, 2 * k) for k in range(1, chips)]
    turned = turn(after(feats, dkv))
    attended, d_queries = finish(kv, probs, dscores)
    stacked = lax.optimization_barrier((*dkv_own, turned, attended, d_queries, upper, lower))
    *dkv_own, turned, attended, d_queries, upper, lower = stacked
    dkv_other = swap(pack(*dkv_own), T, 1)

    halves = 2
    back_out = back(dkv_own, dkv_other, kv_weight, parts, halves)
    d_rows, sent, (columns, dkv_all) = back_out[0], back_out[1:-2], back_out[-2:]
    sent = [swap(x, XY, j + 1) for j, x in enumerate(sent)]
    d_parts = [[d_rows, *sent]]
    for h in range(1, halves):
        d_rows = after(back_rest(dkv_all, kv_weight, h, halves), sent[0])
        d_parts.append([d_rows] + [swap(d_rows, XY, j) for j in range(1, parts)])
    theirs = swap(pack(columns, *sent), T, 1)
    d_kv_weight = kv_grad(
        (projected, aside, across, upper, lower), columns, sent, theirs
    )

    held = None
    for h in range(halves):
        held = weight_grad(turned, d_parts[h], held, h, halves)
    d_weight, d_bias = held
    return attended, d_queries, d_weight, d_bias.reshape(-1), d_kv_weight


def solution(mesh):
    in_specs = (
        P("tensor", ("group", "dp")),
        P(("group", "dp"), "tensor"),
        P("tensor"),
        P("tensor", None),
        P(("group", "dp"), "tensor"),
        P(("group", "dp"), "tensor"),
        P(("group", "dp"), None),
        P(("group", "dp"), None),
    )
    out_specs = (
        P(("group", "dp"), "tensor"),
        P(("group", "dp"), "tensor"),
        P(("group", "dp"), "tensor"),
        P("tensor"),
        P("tensor", ("group", "dp")),
    )
    return jax.shard_map(shards, mesh=mesh, in_specs=in_specs, out_specs=out_specs, check_vma=False)
```

```python
import functools

import jax
import jax.numpy as jnp
from jax import lax
from jax.experimental import pallas as pl
from jax.experimental.pallas import tpu as pltpu
from jax.sharding import PartitionSpec as P

HD = 128

T = "tensor"
XY = ("group", "dp")
F32 = jnp.float32
BF16 = jnp.bfloat16
NT = (((1,), (1,)), ((), ()))
TN = (((0,), (0,)), ((), ()))
VMEM_LIMIT = 8 * 1024 * 1024


def size_of(axes):
    names = axes if isinstance(axes, tuple) else (axes,)
    total = 1
    for name in names:
        total *= lax.axis_size(name)
    return total


def swap(x, axes, bits):
    return lax.ppermute(x, axes, [(i, i ^ bits) for i in range(size_of(axes))])


def after(x, *others):
    return lax.optimization_barrier((x,) + others)[0]


def heads_per_key(queries, kv_weight):
    heads = queries.shape[1] // HD * lax.axis_size(T)
    return heads // (kv_weight.shape[1] // 2 // HD)


def from_partner(shard, axis, distance):
    return lax.ppermute(shard, axis, [(i, i ^ 1 << distance) for i in range(lax.axis_size(axis))])


def general(
    image_feats, proj_weight, proj_bias, kv_weight, queries, out_grad, image_sample, text_sample
):
    gathered = lax.all_gather(image_feats, "tensor", axis=0, tiled=True)
    rows = gathered
    summed = lax.psum_scatter(
        jnp.dot(rows, proj_weight, preferred_element_type=jnp.float32).astype(jnp.bfloat16),
        ("group", "dp"),
        scatter_dimension=0,
        tiled=True,
    ).astype(jnp.float32)
    projected = (summed + proj_bias.astype(jnp.float32)[None, :]).astype(jnp.bfloat16)
    kv_term = jnp.dot(projected, kv_weight, preferred_element_type=jnp.float32)
    kv_all = lax.psum(kv_term, "tensor").astype(jnp.bfloat16)
    local_heads = queries.shape[1] // HD
    shared = heads_per_key(queries, kv_weight)
    half = kv_all.shape[1] // 2
    key_head = lax.axis_index("tensor") * local_heads // shared
    key_start = key_head * HD
    keys = lax.dynamic_slice_in_dim(kv_all, key_start, HD, 1)
    values = lax.dynamic_slice_in_dim(kv_all, key_start + half, HD, 1)
    scale = HD ** (-0.5)
    q_rows = queries.reshape(queries.shape[0], local_heads, HD)
    grads = out_grad.reshape(out_grad.shape[0], local_heads, HD)
    scores = jnp.einsum("thd,id->hti", q_rows, keys, preferred_element_type=jnp.float32) * scale
    allowed = text_sample[0][:, None] == image_sample[0][None, :]
    scores = jnp.where(allowed[None], scores, jnp.float32(-1e30))
    peak = jnp.max(scores, axis=-1, keepdims=True)
    expo = jnp.exp(scores - peak)
    probs = expo / jnp.sum(expo, axis=-1, keepdims=True)
    probs_b = probs.astype(jnp.bfloat16)
    attended = jnp.einsum(
        "hti,id->thd", probs_b, values, preferred_element_type=jnp.float32
    ).astype(jnp.bfloat16)
    dprobs = jnp.einsum("thd,id->hti", grads, values, preferred_element_type=jnp.float32)
    delta = jnp.sum(probs * dprobs, axis=-1, keepdims=True)
    dscores = (probs * (dprobs - delta) * scale).astype(jnp.bfloat16)
    d_rows = jnp.einsum("hti,id->thd", dscores, keys, preferred_element_type=jnp.float32).astype(
        jnp.bfloat16
    )
    d_keys = jnp.einsum("hti,thd->id", dscores, q_rows, preferred_element_type=jnp.float32)
    d_values = jnp.einsum("hti,thd->id", probs_b, grads, preferred_element_type=jnp.float32)
    image_count = kv_term.shape[0]
    members = shared // local_heads
    stacked = jnp.concatenate([d_keys, d_values], axis=1)
    for level in range(members.bit_length() - 1):
        stacked = stacked + from_partner(stacked, "tensor", level)
    width = stacked.shape[1] // members
    member = lax.axis_index("tensor") % members
    mine = lax.dynamic_slice_in_dim(stacked, member * width, width, 1).astype(jnp.bfloat16)
    collected = lax.all_gather(mine, "tensor", axis=1, tiled=True)
    heads_total = collected.shape[1] // (2 * HD)
    dkv = (
        collected.reshape(image_count, heads_total, 2, HD)
        .transpose(0, 2, 1, 3)
        .reshape(image_count, 2 * heads_total * HD)
    )
    d_projected = lax.dot_general(
        dkv, kv_weight, (((1,), (1,)), ((), ())), preferred_element_type=jnp.float32
    ).astype(jnp.bfloat16)
    kv_grad_term = lax.dot_general(
        projected, dkv, (((0,), (0,)), ((), ())), preferred_element_type=jnp.float32
    )
    d_kv_weight = lax.psum_scatter(
        kv_grad_term.astype(jnp.bfloat16), ("group", "dp"), scatter_dimension=1, tiled=True
    )
    piece = lax.all_gather(d_projected, ("group", "dp"), axis=0, tiled=True)
    rows = gathered
    weight_grad = lax.dot_general(
        rows, piece, (((0,), (0,)), ((), ())), preferred_element_type=jnp.float32
    )
    bias_grad = jnp.sum(piece.astype(jnp.float32), axis=0)
    weight_grad, bias_grad = (weight_grad, bias_grad)
    attended = attended.reshape(queries.shape)
    d_queries = d_rows.reshape(queries.shape)
    return (attended, d_queries, weight_grad.astype(jnp.bfloat16), bias_grad, d_kv_weight)


def params():
    return pltpu.CompilerParams(vmem_limit_bytes=VMEM_LIMIT)


def cost(flops, nbytes):
    return pl.CostEstimate(
        flops=flops // 20, bytes_accessed=nbytes // 20, transcendentals=0
    )


def whole(shape):
    return pl.BlockSpec(shape, lambda *_: (0,) * len(shape))


def place_of():
    me = lax.axis_index(T)
    part = lax.axis_index("group") * lax.axis_size("dp") + lax.axis_index("dp")
    return (me // 2) ^ part, me % 2, me, part


def pack_kernel(count, *refs):
    out = refs[-1]
    width = out.shape[2]
    for i, ref in enumerate(refs[:count]):
        out[i] = ref[:, ref.shape[1] - width :]


def pack(*arrays, beside=()):
    rows, width = arrays[0].shape[0], min(x.shape[1] for x in arrays)
    return pl.pallas_call(
        functools.partial(pack_kernel, len(arrays)),
        in_specs=in_vmem(len(arrays)) + [pl.BlockSpec(memory_space=pl.ANY)] * len(beside),
        out_shape=jax.ShapeDtypeStruct((len(arrays), rows, width), BF16),
        compiler_params=params(),
        cost_estimate=cost(0, 8 * len(arrays) * rows * width),
        name="pack",
    )(*arrays, *beside)


def add_kernel(mine, theirs, first, *rest):
    first[...] = mine[0] + theirs[0].astype(F32)
    for k, ref in enumerate(rest):
        ref[...] = (mine[k + 1] + theirs[k + 1].astype(F32)).astype(BF16)


def add(mine, theirs):
    shape = mine.shape[1:]
    return pl.pallas_call(
        add_kernel,
        in_specs=in_vmem(2),
        out_shape=[jax.ShapeDtypeStruct(shape, F32)]
        + [jax.ShapeDtypeStruct(shape, BF16)] * (mine.shape[0] - 1),
        compiler_params=params(),
        cost_estimate=cost(0, 16 * mine.size),
        name="add",
    )(mine, theirs)


def tiles_of(width, tile):
    return width // tile if width % tile == 0 else 1


def project_kernel(groups, *refs):
    place = place_of()
    mine, others = refs[:groups], refs[groups : 2 * groups]
    weight, (partial, feats) = refs[2 * groups], (refs[2 * groups + 1 : -1], refs[-1])
    own = [ref.at[i] for ref in mine for i in range(ref.shape[0])]
    others = [ref.at[i] for ref in others for i in range(ref.shape[0])]
    count = len(own)
    rows = own[0].shape[0]
    for k in range(count):
        j = k ^ place[0]

        @pl.when(place[1] == 0)
        def _():
            feats[j, :rows, :] = own[k][...]
            feats[j, rows:, :] = others[k][...]

        @pl.when(place[1] != 0)
        def _():
            feats[j, :rows, :] = others[k][...]
            feats[j, rows:, :] = own[k][...]

    tiles = tiles_of(weight.shape[1], 256)
    tile = weight.shape[1] // tiles

    def step(n, _):
        at = pl.ds(pl.multiple_of(n * tile, tile), tile)
        lhs = feats[...].reshape(count * 2 * rows, feats.shape[2])
        out = jnp.dot(lhs, weight[:, at], preferred_element_type=F32).astype(BF16)
        for j in range(count):
            partial[j][:, at] = out[j * 2 * rows : (j + 1) * 2 * rows]
        return 0

    lax.fori_loop(0, tiles, step, 0)


def in_vmem(count):
    return [pl.BlockSpec()] * count


def project(own, others, weight):
    count = sum(x.shape[0] for x in own)
    rows, depth = own[0].shape[1:]
    width = weight.shape[1]
    return pl.pallas_call(
        functools.partial(project_kernel, len(own)),
        in_specs=in_vmem(2 * len(own) + 1),
        out_shape=[jax.ShapeDtypeStruct((2 * rows, width), BF16)] * count
        + [jax.ShapeDtypeStruct((count, 2 * rows, depth), BF16)],
        compiler_params=params(),
        cost_estimate=cost(8 * count * rows * depth * width, 2 * depth * width),
        name="project",
    )(*own, *others, weight)


def heads_into(x, place, odd, weight, out):
    half = weight.shape[1] // 2
    for i in range(out.shape[0]):
        start = pl.multiple_of((place[2] ^ (2 * i + odd)) * HD, HD)
        for at, cut in ((start, slice(0, HD)), (half + start, slice(HD, 2 * HD))):
            value = jnp.dot(x, weight[:, pl.ds(at, HD)], preferred_element_type=F32)
            out[i, :, cut] = value.astype(out.dtype)


def combine_kernel(parts, first, *refs):
    place = place_of()
    arrived, (bias, weight, projected, out) = refs[: parts - 1], refs[parts - 1 :]
    total = first[...].astype(F32)
    for ref in arrived:
        total = total + ref[...].astype(F32)
    x = (total + bias[...].astype(F32)).astype(BF16)
    projected[...] = x
    heads_into(x, place, 1, weight, out)


def combine(first, arrived, bias, kv_weight, tensors):
    parts = 1 + len(arrived)
    rows, depth = first.shape
    return pl.pallas_call(
        functools.partial(combine_kernel, parts),
        in_specs=in_vmem(parts + 2),
        out_shape=[
            jax.ShapeDtypeStruct((rows, depth), BF16),
            jax.ShapeDtypeStruct((tensors // 2, rows, 2 * HD), BF16),
        ],
        compiler_params=params(),
        cost_estimate=cost(24 * rows * depth * tensors * HD, depth * tensors * HD * 2),
        name="combine",
    )(first, *arrived, bias, kv_weight)


def own_heads_kernel(projected, weight, out):
    heads_into(projected[...], place_of(), 0, weight, out)


def own_heads(projected, kv_weight, tensors):
    rows, depth = projected.shape
    return pl.pallas_call(
        own_heads_kernel,
        in_specs=in_vmem(2),
        out_shape=jax.ShapeDtypeStruct((tensors // 2, rows, 2 * HD), F32),
        compiler_params=params(),
        cost_estimate=cost(24 * rows * depth * tensors * HD, depth * tensors * HD * 2),
        name="own_heads",
    )(projected, kv_weight)


def attend_kernel(count, *refs):
    first, arrived = refs[0], refs[1:count]
    queries, out_grad, image_ids, text_ids, kv_out, dkv, probs_out, dscores_out = refs[count:]
    total = first[...]
    for ref in arrived:
        total = total + ref[...].astype(F32)
    kv = total.astype(BF16)
    kv_out[...] = kv
    keys, values = kv[:, :HD], kv[:, HD:]
    scale = HD ** (-0.5)
    allowed = image_ids[...] == text_ids[...]
    d_keys = jnp.zeros((kv.shape[0], HD), F32)
    d_values = jnp.zeros((kv.shape[0], HD), F32)
    for head in range(queries.shape[1] // HD):
        at = slice(head * HD, (head + 1) * HD)
        q, g = queries[:, at], out_grad[:, at]
        scores = lax.dot_general(keys, q, NT, preferred_element_type=F32) * scale
        scores = jnp.where(allowed, scores, F32(-1e30))
        expo = jnp.exp(scores - jnp.max(scores, axis=0, keepdims=True))
        probs = expo * (1.0 / jnp.sum(expo, axis=0, keepdims=True))
        probs_b = probs.astype(BF16)
        dprobs = lax.dot_general(values, g, NT, preferred_element_type=F32)
        delta = jnp.sum(probs * dprobs, axis=0, keepdims=True)
        dscores = (probs * (dprobs - delta) * scale).astype(BF16)
        d_keys = d_keys + jnp.dot(dscores, q, preferred_element_type=F32)
        d_values = d_values + jnp.dot(probs_b, g, preferred_element_type=F32)
        probs_out[head] = probs_b
        dscores_out[head] = dscores
    dkv[:, :HD] = d_keys.astype(BF16)
    dkv[:, HD:] = d_values.astype(BF16)


def attend(first, arrived, queries, out_grad, image_ids, text_ids):
    inputs = [first, *arrived, queries, out_grad, image_ids, text_ids]
    shape = first.shape
    heads = queries.shape[1] // HD
    weights = jax.ShapeDtypeStruct((heads, shape[0], queries.shape[0]), BF16)
    return pl.pallas_call(
        functools.partial(attend_kernel, 1 + len(arrived)),
        out_shape=[
            jax.ShapeDtypeStruct(shape, BF16),
            jax.ShapeDtypeStruct(shape, BF16),
            weights,
            weights,
        ],
        compiler_params=params(),
        cost_estimate=cost(16 * 4 * queries.size * shape[0], 8 * queries.size),
        name="attend",
    )(*inputs)


def finish_kernel(kv, probs, dscores, attended, d_queries):
    keys, values = kv[:, :HD], kv[:, HD:]
    for head in range(probs.shape[0]):
        at = slice(head * HD, (head + 1) * HD)
        attended[:, at] = lax.dot_general(
            probs[head], values, TN, preferred_element_type=F32
        ).astype(BF16)
        d_queries[:, at] = lax.dot_general(
            dscores[head], keys, TN, preferred_element_type=F32
        ).astype(BF16)


def finish(kv, probs, dscores):
    heads, images, texts = probs.shape
    out = jax.ShapeDtypeStruct((texts, heads * HD), BF16)
    return pl.pallas_call(
        finish_kernel,
        out_shape=[out, out],
        compiler_params=params(),
        cost_estimate=cost(8 * 4 * heads * images * texts * HD, 8 * probs.size),
        name="finish",
    )(kv, probs, dscores)


def turn_kernel(feats, out):
    parts, rows, tile = feats.shape
    out[...] = feats[...].reshape(parts * rows, tile).T


def turn(feats):
    parts, rows, depth = feats.shape
    tile = depth // tiles_of(depth, 640)
    total = parts * rows
    return pl.pallas_call(
        turn_kernel,
        grid=(depth // tile,),
        in_specs=[pl.BlockSpec((parts, rows, tile), lambda n: (0, 0, n))],
        out_specs=pl.BlockSpec((tile, total), lambda n: (n, 0)),
        out_shape=jax.ShapeDtypeStruct((depth, total), BF16),
        compiler_params=params(),
        cost_estimate=cost(0, 8 * depth * total),
        name="turn",
    )(feats)


def back_columns(dkv, weight, first, targets):
    columns = targets[0].shape[1]
    count = tiles_of(columns, 256)
    tile = columns // count
    for n in range(count):
        value = lax.dot_general(
            dkv,
            weight[first + n * tile : first + (n + 1) * tile, :],
            NT,
            preferred_element_type=F32,
        ).astype(BF16)
        for ref in targets:
            ref[:, n * tile : (n + 1) * tile] = value


def back_kernel(chips, *refs):
    place = place_of()
    own, (other, weight, out), refs = refs[:chips], refs[chips : chips + 3], refs[chips + 3 :]
    sent, (cols, dkv_all) = refs[:-2], refs[-2:]
    columns = out.shape[1]
    half = dkv_all.shape[1] // 2
    for k in range(chips):
        for block, bits in ((own[k][...], 2 * k), (other[k], 2 * k + 1)):
            start = pl.multiple_of((place[2] ^ bits) * HD, HD)
            dkv_all[:, pl.ds(start, HD)] = block[:, :HD]
            dkv_all[:, pl.ds(half + start, HD)] = block[:, HD:]
    width = cols.shape[1] * 2
    for j in range(len(sent) + 1):
        for m in range(width // HD // 2):
            start = (place[3] ^ j) * width + (2 * m + place[1]) * HD
            block = dkv_all[:, pl.ds(pl.multiple_of(start, HD), HD)]
            at = slice(m * HD, (m + 1) * HD)
            if j == 0:
                cols[:, at] = block
            else:
                sent[j - 1][:, columns + m * HD : columns + (m + 1) * HD] = block
    back_columns(dkv_all[...], weight, 0, [out])
    for ref in sent:
        ref[:, :columns] = out[...]


def back(own, other, kv_weight, parts):
    rows = own[0].shape[0]
    depth, width = kv_weight.shape
    columns = depth
    extra = width // parts // 2
    full = jax.ShapeDtypeStruct((rows, columns + extra), BF16)
    return pl.pallas_call(
        functools.partial(back_kernel, len(own)),
        in_specs=in_vmem(len(own) + 2),
        out_shape=[jax.ShapeDtypeStruct((rows, columns), BF16)]
        + [full] * (parts - 1)
        + [
            jax.ShapeDtypeStruct((rows, extra), BF16),
            jax.ShapeDtypeStruct((rows, width), BF16),
        ],
        compiler_params=params(),
        cost_estimate=cost(8 * rows * columns * width, 2 * columns * width),
        name="back",
    )(*own, other, kv_weight)


def kv_grad_kernel(count, parts, *refs):
    place = place_of()
    left, mine, (theirs, out, right) = refs[:count], refs[count : count + parts], refs[-3:]
    rows = left[0].shape[0]
    extra = mine[0].shape[1]
    for j in range(parts):
        at = slice(j * rows, (j + 1) * rows)
        skip = mine[j].shape[1] - extra
        for m in range(extra // HD):
            start = pl.multiple_of((2 * m + place[1]) * HD, HD)
            right[at, pl.ds(start, HD)] = mine[j][:, skip + m * HD : skip + (m + 1) * HD]
            start = pl.multiple_of((2 * m + 1 - place[1]) * HD, HD)
            right[at, pl.ds(start, HD)] = theirs[j, :, m * HD : (m + 1) * HD]
    depth = out.shape[0]
    count = tiles_of(depth, 256)
    tile = depth // count
    for n in range(count):
        at = slice(n * tile, (n + 1) * tile)
        lhs = jnp.concatenate([x[:, at] for x in left], axis=0)
        out[at, :] = lax.dot_general(
            lhs, right[...], TN, preferred_element_type=F32
        ).astype(BF16)


def kv_grad(left, own, sent, theirs):
    parts = 1 + len(sent)
    rows, depth = left[0].shape
    extra = own.shape[1]
    return pl.pallas_call(
        functools.partial(kv_grad_kernel, len(left), parts),
        in_specs=in_vmem(len(left) + parts + 1),
        out_shape=jax.ShapeDtypeStruct((depth, 2 * extra), BF16),
        scratch_shapes=[pltpu.VMEM((parts * rows, 2 * extra), BF16)],
        compiler_params=params(),
        cost_estimate=cost(4 * parts * rows * depth * extra, 4 * parts * rows * depth),
        name="kv_grad",
    )(*left, own, *sent, theirs)


def side_by_side(grads, right):
    total = None
    rows, columns = grads[0].shape[0], right.shape[1]
    for i, ref in enumerate(grads):
        value = ref[:, :columns]
        right[i * rows : (i + 1) * rows, :] = value
        term = jnp.sum(value.astype(F32), axis=0, keepdims=True)
        total = term if total is None else total + term
    return total


def first_grad_kernel(count, feats, *refs):
    grads, (out, bias, right) = refs[:count], refs[count:]
    bias[...] = side_by_side(grads, right)
    tiles = tiles_of(out.shape[0], 384)
    tile = out.shape[0] // tiles
    for n in range(tiles):
        at = slice(n * tile, (n + 1) * tile)
        out[at, :] = jnp.dot(
            feats[at, : right.shape[0]], right[...], preferred_element_type=F32
        )


def first_grad(feats, grads):
    depth = feats.shape[0]
    rows, columns = grads[0].shape
    total = len(grads) * rows
    return pl.pallas_call(
        functools.partial(first_grad_kernel, len(grads)),
        in_specs=in_vmem(1 + len(grads)),
        out_shape=[
            jax.ShapeDtypeStruct((depth, columns), F32),
            jax.ShapeDtypeStruct((1, columns), F32),
        ],
        scratch_shapes=[pltpu.VMEM((total, columns), BF16)],
        compiler_params=params(),
        cost_estimate=cost(2 * total * depth * columns, 4 * depth * columns),
        name="first_grad",
    )(feats, *grads)


def last_grad_kernel(count, feats, before, bias_before, *refs):
    grads, (out, bias, right, rounded, sems) = refs[:count], refs[count:]
    bias[...] = bias_before[...] + side_by_side(grads, right)
    tiles = tiles_of(out.shape[0], 384)
    tile = out.shape[0] // tiles
    skip = feats.shape[1] - right.shape[0]
    copies = []
    for n in range(tiles):
        at = pl.ds(n * tile, tile)
        value = before[at, :] + jnp.dot(
            feats[at, skip:], right[...], preferred_element_type=F32
        )
        rounded[at, :] = value.astype(BF16)
        copy = pltpu.make_async_copy(rounded.at[at, :], out.at[at, :], sems.at[n])
        copy.start()
        copies.append(copy)
    for copy in copies:
        copy.wait()


def last_grad(feats, before, bias, grads):
    depth, columns = before.shape
    total = len(grads) * grads[0].shape[0]
    return pl.pallas_call(
        functools.partial(last_grad_kernel, len(grads)),
        in_specs=in_vmem(3 + len(grads)),
        out_specs=[pl.BlockSpec(memory_space=pl.ANY), pl.BlockSpec()],
        out_shape=[
            jax.ShapeDtypeStruct((depth, columns), BF16),
            jax.ShapeDtypeStruct((1, columns), F32),
        ],
        scratch_shapes=[
            pltpu.VMEM((total, columns), BF16),
            pltpu.VMEM((depth, columns), BF16),
            pltpu.SemaphoreType.DMA((tiles_of(depth, 384),)),
        ],
        compiler_params=params(),
        cost_estimate=cost(2 * total * depth * columns, 6 * depth * columns),
        name="last_grad",
    )(feats, before, bias, *grads)


def shards(
    image_feats, proj_weight, proj_bias, kv_weight, queries, out_grad, image_sample, text_sample
):
    tensors = lax.axis_size(T)
    chips = tensors // 2
    parts = size_of(XY)
    if (
        heads_per_key(queries, kv_weight) * HD != queries.shape[1]
        or chips != parts
        or parts != 4
    ):
        return general(
            image_feats, proj_weight, proj_bias, kv_weight, queries, out_grad, image_sample, text_sample
        )
    own = [image_feats] + [swap(image_feats, T, 2 * k) for k in range(1, chips)]
    image_ids = after(image_sample, own[1]).reshape(-1, 1)
    stacks = [pack(*own[: chips // 2], beside=(proj_weight,)), pack(*own[chips // 2 :])]
    *partial, feats = project(stacks, [swap(x, T, 1) for x in stacks], proj_weight)
    arrived = [swap(partial[j], XY, j) for j in range(1, parts)]

    projected, theirs = combine(
        partial[0], arrived, proj_bias.reshape(1, -1), kv_weight, tensors
    )
    theirs = swap(theirs, T, 1)
    mine = own_heads(projected, kv_weight, tensors)
    mine, *kv_sent = add(mine, theirs)
    kv_parts = [swap(x, T, 2 * k) for k, x in enumerate(kv_sent, 1)]
    ready = after(projected, *kv_sent)
    aside, across = swap(ready, XY, 1), swap(ready, XY, 2)
    *kv_parts, aside, across = lax.optimization_barrier((*kv_parts, aside, across))

    kv, dkv, probs, dscores = attend(
        mine, kv_parts, queries, out_grad, image_ids, text_sample
    )
    cut = projected.shape[0] // 2
    upper, lower, _ = lax.optimization_barrier((across[:cut], aside[cut:], dkv))
    upper, lower = swap(upper, XY, 1), swap(lower, XY, 2)
    dkv_own = [dkv] + [swap(dkv, T, 2 * k) for k in range(1, chips)]
    turned = turn(after(feats, dkv))
    attended, d_queries = finish(kv, probs, dscores)
    stacked = lax.optimization_barrier((*dkv_own, turned, attended, d_queries, upper, lower))
    *dkv_own, turned, attended, d_queries, upper, lower = stacked
    dkv_other = swap(pack(*dkv_own), T, 1)

    back_out = back(dkv_own, dkv_other, kv_weight, parts)
    d_rows, sent, columns = back_out[0], back_out[1:-2], back_out[-2]
    sent = [swap(x, XY, j + 1) for j, x in enumerate(sent)]
    early = parts // 2
    partial, bias = first_grad(turned, [d_rows] + sent[: early - 1])
    d_weight, d_bias = last_grad(turned, partial, bias, sent[early - 1 :])
    ours = lax.optimization_barrier((columns, *sent, bias))[:-1]
    theirs = swap(pack(*ours), T, 1)
    d_kv_weight = kv_grad(
        (projected, aside, across, upper, lower), columns, sent, theirs
    )
    return attended, d_queries, d_weight, d_bias.reshape(-1), d_kv_weight


def solution(mesh):
    in_specs = (
        P("tensor", ("group", "dp")),
        P(("group", "dp"), "tensor"),
        P("tensor"),
        P("tensor", None),
        P(("group", "dp"), "tensor"),
        P(("group", "dp"), "tensor"),
        P(("group", "dp"), None),
        P(("group", "dp"), None),
    )
    out_specs = (
        P(("group", "dp"), "tensor"),
        P(("group", "dp"), "tensor"),
        P(("group", "dp"), "tensor"),
        P("tensor"),
        P("tensor", ("group", "dp")),
    )
    return jax.shard_map(shards, mesh=mesh, in_specs=in_specs, out_specs=out_specs, check_vma=False)
```

```python
import functools

import jax
import jax.numpy as jnp
from jax import lax
from jax.experimental import pallas as pl
from jax.experimental.pallas import tpu as pltpu
from jax.sharding import PartitionSpec as P

HD = 128

T = "tensor"
XY = ("group", "dp")
F32 = jnp.float32
BF16 = jnp.bfloat16
NT = (((1,), (1,)), ((), ()))
TN = (((0,), (0,)), ((), ()))
VMEM_LIMIT = 8 * 1024 * 1024


def size_of(axes):
    names = axes if isinstance(axes, tuple) else (axes,)
    total = 1
    for name in names:
        total *= lax.axis_size(name)
    return total


def swap(x, axes, bits):
    return lax.ppermute(x, axes, [(i, i ^ bits) for i in range(size_of(axes))])


def after(x, *others):
    return lax.optimization_barrier((x,) + others)[0]


def heads_per_key(queries, kv_weight):
    heads = queries.shape[1] // HD * lax.axis_size(T)
    return heads // (kv_weight.shape[1] // 2 // HD)


def from_partner(shard, axis, distance):
    return lax.ppermute(shard, axis, [(i, i ^ 1 << distance) for i in range(lax.axis_size(axis))])


def general(
    image_feats, proj_weight, proj_bias, kv_weight, queries, out_grad, image_sample, text_sample
):
    gathered = lax.all_gather(image_feats, "tensor", axis=0, tiled=True)
    rows = gathered
    summed = lax.psum_scatter(
        jnp.dot(rows, proj_weight, preferred_element_type=jnp.float32).astype(jnp.bfloat16),
        ("group", "dp"),
        scatter_dimension=0,
        tiled=True,
    ).astype(jnp.float32)
    projected = (summed + proj_bias.astype(jnp.float32)[None, :]).astype(jnp.bfloat16)
    kv_term = jnp.dot(projected, kv_weight, preferred_element_type=jnp.float32)
    kv_all = lax.psum(kv_term, "tensor").astype(jnp.bfloat16)
    local_heads = queries.shape[1] // HD
    shared = heads_per_key(queries, kv_weight)
    half = kv_all.shape[1] // 2
    key_head = lax.axis_index("tensor") * local_heads // shared
    key_start = key_head * HD
    keys = lax.dynamic_slice_in_dim(kv_all, key_start, HD, 1)
    values = lax.dynamic_slice_in_dim(kv_all, key_start + half, HD, 1)
    scale = HD ** (-0.5)
    q_rows = queries.reshape(queries.shape[0], local_heads, HD)
    grads = out_grad.reshape(out_grad.shape[0], local_heads, HD)
    scores = jnp.einsum("thd,id->hti", q_rows, keys, preferred_element_type=jnp.float32) * scale
    allowed = text_sample[0][:, None] == image_sample[0][None, :]
    scores = jnp.where(allowed[None], scores, jnp.float32(-1e30))
    peak = jnp.max(scores, axis=-1, keepdims=True)
    expo = jnp.exp(scores - peak)
    probs = expo / jnp.sum(expo, axis=-1, keepdims=True)
    probs_b = probs.astype(jnp.bfloat16)
    attended = jnp.einsum(
        "hti,id->thd", probs_b, values, preferred_element_type=jnp.float32
    ).astype(jnp.bfloat16)
    dprobs = jnp.einsum("thd,id->hti", grads, values, preferred_element_type=jnp.float32)
    delta = jnp.sum(probs * dprobs, axis=-1, keepdims=True)
    dscores = (probs * (dprobs - delta) * scale).astype(jnp.bfloat16)
    d_rows = jnp.einsum("hti,id->thd", dscores, keys, preferred_element_type=jnp.float32).astype(
        jnp.bfloat16
    )
    d_keys = jnp.einsum("hti,thd->id", dscores, q_rows, preferred_element_type=jnp.float32)
    d_values = jnp.einsum("hti,thd->id", probs_b, grads, preferred_element_type=jnp.float32)
    image_count = kv_term.shape[0]
    members = shared // local_heads
    stacked = jnp.concatenate([d_keys, d_values], axis=1)
    for level in range(members.bit_length() - 1):
        stacked = stacked + from_partner(stacked, "tensor", level)
    width = stacked.shape[1] // members
    member = lax.axis_index("tensor") % members
    mine = lax.dynamic_slice_in_dim(stacked, member * width, width, 1).astype(jnp.bfloat16)
    collected = lax.all_gather(mine, "tensor", axis=1, tiled=True)
    heads_total = collected.shape[1] // (2 * HD)
    dkv = (
        collected.reshape(image_count, heads_total, 2, HD)
        .transpose(0, 2, 1, 3)
        .reshape(image_count, 2 * heads_total * HD)
    )
    d_projected = lax.dot_general(
        dkv, kv_weight, (((1,), (1,)), ((), ())), preferred_element_type=jnp.float32
    ).astype(jnp.bfloat16)
    kv_grad_term = lax.dot_general(
        projected, dkv, (((0,), (0,)), ((), ())), preferred_element_type=jnp.float32
    )
    d_kv_weight = lax.psum_scatter(
        kv_grad_term.astype(jnp.bfloat16), ("group", "dp"), scatter_dimension=1, tiled=True
    )
    piece = lax.all_gather(d_projected, ("group", "dp"), axis=0, tiled=True)
    rows = gathered
    weight_grad = lax.dot_general(
        rows, piece, (((0,), (0,)), ((), ())), preferred_element_type=jnp.float32
    )
    bias_grad = jnp.sum(piece.astype(jnp.float32), axis=0)
    weight_grad, bias_grad = (weight_grad, bias_grad)
    attended = attended.reshape(queries.shape)
    d_queries = d_rows.reshape(queries.shape)
    return (attended, d_queries, weight_grad.astype(jnp.bfloat16), bias_grad, d_kv_weight)


def params():
    return pltpu.CompilerParams(vmem_limit_bytes=VMEM_LIMIT)


def cost(flops, nbytes):
    return pl.CostEstimate(
        flops=flops // 20, bytes_accessed=nbytes // 20, transcendentals=0
    )


def whole(shape):
    return pl.BlockSpec(shape, lambda *_: (0,) * len(shape))


def place_of():
    me = lax.axis_index(T)
    part = lax.axis_index("group") * lax.axis_size("dp") + lax.axis_index("dp")
    return (me // 2) ^ part, me % 2, me, part


def pack_kernel(count, *refs):
    out = refs[-1]
    width = out.shape[2]
    for i, ref in enumerate(refs[:count]):
        out[i] = ref[:, ref.shape[1] - width :]


def pack(*arrays, beside=()):
    rows, width = arrays[0].shape[0], min(x.shape[1] for x in arrays)
    return pl.pallas_call(
        functools.partial(pack_kernel, len(arrays)),
        in_specs=in_vmem(len(arrays)) + [pl.BlockSpec(memory_space=pl.ANY)] * len(beside),
        out_shape=jax.ShapeDtypeStruct((len(arrays), rows, width), BF16),
        compiler_params=params(),
        cost_estimate=cost(0, 8 * len(arrays) * rows * width),
        name="pack",
    )(*arrays, *beside)


def add_kernel(mine, theirs, first, *rest):
    first[...] = mine[0] + theirs[0].astype(F32)
    for k, ref in enumerate(rest):
        ref[...] = (mine[k + 1] + theirs[k + 1].astype(F32)).astype(BF16)


def add(mine, theirs):
    shape = mine.shape[1:]
    return pl.pallas_call(
        add_kernel,
        in_specs=in_vmem(2),
        out_shape=[jax.ShapeDtypeStruct(shape, F32)]
        + [jax.ShapeDtypeStruct(shape, BF16)] * (mine.shape[0] - 1),
        compiler_params=params(),
        cost_estimate=cost(0, 16 * mine.size),
        name="add",
    )(mine, theirs)


def tiles_of(width, tile):
    return width // tile if width % tile == 0 else 1


def project_kernel(groups, *refs):
    place = place_of()
    mine, others = refs[:groups], refs[groups : 2 * groups]
    weight, (partial, feats) = refs[2 * groups], (refs[2 * groups + 1 : -1], refs[-1])
    own = [ref.at[i] for ref in mine for i in range(ref.shape[0])]
    others = [ref.at[i] for ref in others for i in range(ref.shape[0])]
    count = len(own)
    rows = own[0].shape[0]
    for k in range(count):
        j = k ^ place[0]

        @pl.when(place[1] == 0)
        def _():
            feats[j, :rows, :] = own[k][...]
            feats[j, rows:, :] = others[k][...]

        @pl.when(place[1] != 0)
        def _():
            feats[j, :rows, :] = others[k][...]
            feats[j, rows:, :] = own[k][...]

    tiles = tiles_of(weight.shape[1], 256)
    tile = weight.shape[1] // tiles

    def step(n, _):
        at = pl.ds(pl.multiple_of(n * tile, tile), tile)
        lhs = feats[...].reshape(count * 2 * rows, feats.shape[2])
        out = jnp.dot(lhs, weight[:, at], preferred_element_type=F32).astype(BF16)
        for j in range(count):
            partial[j][:, at] = out[j * 2 * rows : (j + 1) * 2 * rows]
        return 0

    lax.fori_loop(0, tiles, step, 0)


def in_vmem(count):
    return [pl.BlockSpec()] * count


def project(own, others, weight):
    count = sum(x.shape[0] for x in own)
    rows, depth = own[0].shape[1:]
    width = weight.shape[1]
    return pl.pallas_call(
        functools.partial(project_kernel, len(own)),
        in_specs=in_vmem(2 * len(own) + 1),
        out_shape=[jax.ShapeDtypeStruct((2 * rows, width), BF16)] * count
        + [jax.ShapeDtypeStruct((count, 2 * rows, depth), BF16)],
        compiler_params=params(),
        cost_estimate=cost(8 * count * rows * depth * width, 2 * depth * width),
        name="project",
    )(*own, *others, weight)


def heads_into(x, place, odd, weight, out):
    half = weight.shape[1] // 2
    for i in range(out.shape[0]):
        start = pl.multiple_of((place[2] ^ (2 * i + odd)) * HD, HD)
        for at, cut in ((start, slice(0, HD)), (half + start, slice(HD, 2 * HD))):
            value = jnp.dot(x, weight[:, pl.ds(at, HD)], preferred_element_type=F32)
            out[i, :, cut] = value.astype(out.dtype)


def combine_kernel(parts, first, *refs):
    place = place_of()
    arrived, (bias, weight, projected, out) = refs[: parts - 1], refs[parts - 1 :]
    total = first[...].astype(F32)
    for ref in arrived:
        total = total + ref[...].astype(F32)
    x = (total + bias[...].astype(F32)).astype(BF16)
    projected[...] = x
    heads_into(x, place, 1, weight, out)


def combine(first, arrived, bias, kv_weight, tensors):
    parts = 1 + len(arrived)
    rows, depth = first.shape
    return pl.pallas_call(
        functools.partial(combine_kernel, parts),
        in_specs=in_vmem(parts + 2),
        out_shape=[
            jax.ShapeDtypeStruct((rows, depth), BF16),
            jax.ShapeDtypeStruct((tensors // 2, rows, 2 * HD), BF16),
        ],
        compiler_params=params(),
        cost_estimate=cost(24 * rows * depth * tensors * HD, depth * tensors * HD * 2),
        name="combine",
    )(first, *arrived, bias, kv_weight)


def own_heads_kernel(projected, weight, out):
    heads_into(projected[...], place_of(), 0, weight, out)


def own_heads(projected, kv_weight, tensors):
    rows, depth = projected.shape
    return pl.pallas_call(
        own_heads_kernel,
        in_specs=in_vmem(2),
        out_shape=jax.ShapeDtypeStruct((tensors // 2, rows, 2 * HD), F32),
        compiler_params=params(),
        cost_estimate=cost(24 * rows * depth * tensors * HD, depth * tensors * HD * 2),
        name="own_heads",
    )(projected, kv_weight)


def attend_kernel(count, *refs):
    first, arrived = refs[0], refs[1:count]
    queries, out_grad, image_ids, text_ids, kv_out, dkv, probs_out, dscores_out = refs[count:]
    total = first[...]
    for ref in arrived:
        total = total + ref[...].astype(F32)
    kv = total.astype(BF16)
    kv_out[...] = kv
    keys, values = kv[:, :HD], kv[:, HD:]
    scale = HD ** (-0.5)
    allowed = image_ids[...] == text_ids[...]
    d_keys = jnp.zeros((kv.shape[0], HD), F32)
    d_values = jnp.zeros((kv.shape[0], HD), F32)
    for head in range(queries.shape[1] // HD):
        at = slice(head * HD, (head + 1) * HD)
        q, g = queries[:, at], out_grad[:, at]
        scores = lax.dot_general(keys, q, NT, preferred_element_type=F32) * scale
        scores = jnp.where(allowed, scores, F32(-1e30))
        expo = jnp.exp(scores - jnp.max(scores, axis=0, keepdims=True))
        probs = expo * (1.0 / jnp.sum(expo, axis=0, keepdims=True))
        probs_b = probs.astype(BF16)
        dprobs = lax.dot_general(values, g, NT, preferred_element_type=F32)
        delta = jnp.sum(probs * dprobs, axis=0, keepdims=True)
        dscores = (probs * (dprobs - delta) * scale).astype(BF16)
        d_keys = d_keys + jnp.dot(dscores, q, preferred_element_type=F32)
        d_values = d_values + jnp.dot(probs_b, g, preferred_element_type=F32)
        probs_out[head] = probs_b
        dscores_out[head] = dscores
    dkv[:, :HD] = d_keys.astype(BF16)
    dkv[:, HD:] = d_values.astype(BF16)


def attend(first, arrived, queries, out_grad, image_ids, text_ids):
    inputs = [first, *arrived, queries, out_grad, image_ids, text_ids]
    shape = first.shape
    heads = queries.shape[1] // HD
    weights = jax.ShapeDtypeStruct((heads, shape[0], queries.shape[0]), BF16)
    return pl.pallas_call(
        functools.partial(attend_kernel, 1 + len(arrived)),
        out_shape=[
            jax.ShapeDtypeStruct(shape, BF16),
            jax.ShapeDtypeStruct(shape, BF16),
            weights,
            weights,
        ],
        compiler_params=params(),
        cost_estimate=cost(16 * 4 * queries.size * shape[0], 8 * queries.size),
        name="attend",
    )(*inputs)


def finish_kernel(kv, probs, dscores, attended, d_queries):
    keys, values = kv[:, :HD], kv[:, HD:]
    for head in range(probs.shape[0]):
        at = slice(head * HD, (head + 1) * HD)
        attended[:, at] = lax.dot_general(
            probs[head], values, TN, preferred_element_type=F32
        ).astype(BF16)
        d_queries[:, at] = lax.dot_general(
            dscores[head], keys, TN, preferred_element_type=F32
        ).astype(BF16)


def finish(kv, probs, dscores):
    heads, images, texts = probs.shape
    out = jax.ShapeDtypeStruct((texts, heads * HD), BF16)
    return pl.pallas_call(
        finish_kernel,
        out_shape=[out, out],
        compiler_params=params(),
        cost_estimate=cost(8 * 4 * heads * images * texts * HD, 8 * probs.size),
        name="finish",
    )(kv, probs, dscores)


def turn_kernel(feats, out):
    parts, rows, tile = feats.shape
    out[...] = feats[...].reshape(parts * rows, tile).T


def turn(feats):
    parts, rows, depth = feats.shape
    tile = depth // tiles_of(depth, 640)
    total = parts * rows
    return pl.pallas_call(
        turn_kernel,
        grid=(depth // tile,),
        in_specs=[pl.BlockSpec((parts, rows, tile), lambda n: (0, 0, n))],
        out_specs=pl.BlockSpec((tile, total), lambda n: (n, 0)),
        out_shape=jax.ShapeDtypeStruct((depth, total), BF16),
        compiler_params=params(),
        cost_estimate=cost(0, 8 * depth * total),
        name="turn",
    )(feats)


def back_columns(dkv, weight, first, targets):
    columns = targets[0].shape[1]
    count = tiles_of(columns, 256)
    tile = columns // count
    for n in range(count):
        value = lax.dot_general(
            dkv,
            weight[first + n * tile : first + (n + 1) * tile, :],
            NT,
            preferred_element_type=F32,
        ).astype(BF16)
        for ref in targets:
            ref[:, n * tile : (n + 1) * tile] = value


def back_kernel(chips, *refs):
    place = place_of()
    own, (other, weight, out), refs = refs[:chips], refs[chips : chips + 3], refs[chips + 3 :]
    sent, (cols, dkv_all) = refs[:-2], refs[-2:]
    columns = out.shape[1]
    half = dkv_all.shape[1] // 2
    for k in range(chips):
        for block, bits in ((own[k][...], 2 * k), (other[k], 2 * k + 1)):
            start = pl.multiple_of((place[2] ^ bits) * HD, HD)
            dkv_all[:, pl.ds(start, HD)] = block[:, :HD]
            dkv_all[:, pl.ds(half + start, HD)] = block[:, HD:]
    width = cols.shape[1] * 2
    for j in range(len(sent) + 1):
        for m in range(width // HD // 2):
            start = (place[3] ^ j) * width + (2 * m + place[1]) * HD
            block = dkv_all[:, pl.ds(pl.multiple_of(start, HD), HD)]
            at = slice(m * HD, (m + 1) * HD)
            if j == 0:
                cols[:, at] = block
            else:
                sent[j - 1][:, columns + m * HD : columns + (m + 1) * HD] = block
    back_columns(dkv_all[...], weight, 0, [out])
    for ref in sent:
        ref[:, :columns] = out[...]


def back(own, other, kv_weight, parts):
    rows = own[0].shape[0]
    depth, width = kv_weight.shape
    columns = depth
    extra = width // parts // 2
    full = jax.ShapeDtypeStruct((rows, columns + extra), BF16)
    return pl.pallas_call(
        functools.partial(back_kernel, len(own)),
        in_specs=in_vmem(len(own) + 2),
        out_shape=[jax.ShapeDtypeStruct((rows, columns), BF16)]
        + [full] * (parts - 1)
        + [
            jax.ShapeDtypeStruct((rows, extra), BF16),
            jax.ShapeDtypeStruct((rows, width), BF16),
        ],
        compiler_params=params(),
        cost_estimate=cost(8 * rows * columns * width, 2 * columns * width),
        name="back",
    )(*own, other, kv_weight)


def kv_grad_kernel(count, parts, *refs):
    place = place_of()
    left, mine = refs[:count], refs[count : count + parts]
    theirs, out, right, rounded, sems = refs[count + parts :]
    rows = left[0].shape[0]
    extra = mine[0].shape[1]
    for j in range(parts):
        at = slice(j * rows, (j + 1) * rows)
        skip = mine[j].shape[1] - extra
        for m in range(extra // HD):
            start = pl.multiple_of((2 * m + place[1]) * HD, HD)
            right[at, pl.ds(start, HD)] = mine[j][:, skip + m * HD : skip + (m + 1) * HD]
            start = pl.multiple_of((2 * m + 1 - place[1]) * HD, HD)
            right[at, pl.ds(start, HD)] = theirs[j, :, m * HD : (m + 1) * HD]
    depth = out.shape[0]
    count = tiles_of(depth, 256)
    tile = depth // count
    copies = []
    for n in range(count):
        at = slice(n * tile, (n + 1) * tile)
        lhs = jnp.concatenate([x[:, at] for x in left], axis=0)
        rounded[at, :] = lax.dot_general(
            lhs, right[...], TN, preferred_element_type=F32
        ).astype(BF16)
        rows_at = pl.ds(n * tile, tile)
        copy = pltpu.make_async_copy(
            rounded.at[rows_at, :], out.at[rows_at, :], sems.at[n]
        )
        copy.start()
        copies.append(copy)
    for copy in copies:
        copy.wait()


def kv_grad(left, own, sent, theirs):
    parts = 1 + len(sent)
    rows, depth = left[0].shape
    extra = own.shape[1]
    return pl.pallas_call(
        functools.partial(kv_grad_kernel, len(left), parts),
        in_specs=in_vmem(len(left) + parts + 1),
        out_shape=jax.ShapeDtypeStruct((depth, 2 * extra), BF16),
        out_specs=pl.BlockSpec(memory_space=pl.ANY),
        scratch_shapes=[
            pltpu.VMEM((parts * rows, 2 * extra), BF16),
            pltpu.VMEM((depth, 2 * extra), BF16),
            pltpu.SemaphoreType.DMA((tiles_of(depth, 256),)),
        ],
        compiler_params=params(),
        cost_estimate=cost(4 * parts * rows * depth * extra, 4 * parts * rows * depth),
        name="kv_grad",
    )(*left, own, *sent, theirs)


def side_by_side(grads, right):
    total = None
    rows, columns = grads[0].shape[0], right.shape[1]
    for i, ref in enumerate(grads):
        value = ref[:, :columns]
        right[i * rows : (i + 1) * rows, :] = value
        term = jnp.sum(value.astype(F32), axis=0, keepdims=True)
        total = term if total is None else total + term
    return total


def first_grad_kernel(count, feats, *refs):
    grads, (out, bias, right) = refs[:count], refs[count:]
    bias[...] = side_by_side(grads, right)
    tiles = tiles_of(out.shape[0], 384)
    tile = out.shape[0] // tiles
    for n in range(tiles):
        at = slice(n * tile, (n + 1) * tile)
        out[at, :] = jnp.dot(
            feats[at, : right.shape[0]], right[...], preferred_element_type=F32
        )


def first_grad(feats, grads):
    depth = feats.shape[0]
    rows, columns = grads[0].shape
    total = len(grads) * rows
    return pl.pallas_call(
        functools.partial(first_grad_kernel, len(grads)),
        in_specs=in_vmem(1 + len(grads)),
        out_shape=[
            jax.ShapeDtypeStruct((depth, columns), F32),
            jax.ShapeDtypeStruct((1, columns), F32),
        ],
        scratch_shapes=[pltpu.VMEM((total, columns), BF16)],
        compiler_params=params(),
        cost_estimate=cost(2 * total * depth * columns, 4 * depth * columns),
        name="first_grad",
    )(feats, *grads)


def last_grad_kernel(count, feats, before, bias_before, *refs):
    grads, (out, bias, right, rounded, sems) = refs[:count], refs[count:]
    bias[...] = bias_before[...] + side_by_side(grads, right)
    tiles = tiles_of(out.shape[0], 384)
    tile = out.shape[0] // tiles
    skip = feats.shape[1] - right.shape[0]
    copies = []
    for n in range(tiles):
        at = pl.ds(n * tile, tile)
        value = before[at, :] + jnp.dot(
            feats[at, skip:], right[...], preferred_element_type=F32
        )
        rounded[at, :] = value.astype(BF16)
        copy = pltpu.make_async_copy(rounded.at[at, :], out.at[at, :], sems.at[n])
        copy.start()
        copies.append(copy)
    for copy in copies:
        copy.wait()


def last_grad(feats, before, bias, grads):
    depth, columns = before.shape
    total = len(grads) * grads[0].shape[0]
    return pl.pallas_call(
        functools.partial(last_grad_kernel, len(grads)),
        in_specs=in_vmem(3 + len(grads)),
        out_specs=[pl.BlockSpec(memory_space=pl.ANY), pl.BlockSpec()],
        out_shape=[
            jax.ShapeDtypeStruct((depth, columns), BF16),
            jax.ShapeDtypeStruct((1, columns), F32),
        ],
        scratch_shapes=[
            pltpu.VMEM((total, columns), BF16),
            pltpu.VMEM((depth, columns), BF16),
            pltpu.SemaphoreType.DMA((tiles_of(depth, 384),)),
        ],
        compiler_params=params(),
        cost_estimate=cost(2 * total * depth * columns, 6 * depth * columns),
        name="last_grad",
    )(feats, before, bias, *grads)


def shards(
    image_feats, proj_weight, proj_bias, kv_weight, queries, out_grad, image_sample, text_sample
):
    tensors = lax.axis_size(T)
    chips = tensors // 2
    parts = size_of(XY)
    if (
        heads_per_key(queries, kv_weight) * HD != queries.shape[1]
        or chips != parts
        or parts != 4
    ):
        return general(
            image_feats, proj_weight, proj_bias, kv_weight, queries, out_grad, image_sample, text_sample
        )
    own = [image_feats] + [swap(image_feats, T, 2 * k) for k in range(1, chips)]
    image_ids = after(image_sample, own[1]).reshape(-1, 1)
    stacks = [pack(*own[: chips // 2], beside=(proj_weight,)), pack(*own[chips // 2 :])]
    *partial, feats = project(stacks, [swap(x, T, 1) for x in stacks], proj_weight)
    arrived = [swap(partial[j], XY, j) for j in range(1, parts)]

    projected, theirs = combine(
        partial[0], arrived, proj_bias.reshape(1, -1), kv_weight, tensors
    )
    theirs = swap(theirs, T, 1)
    mine = own_heads(projected, kv_weight, tensors)
    mine, *kv_sent = add(mine, theirs)
    kv_parts = [swap(x, T, 2 * k) for k, x in enumerate(kv_sent, 1)]
    ready = after(projected, *kv_sent)
    aside, across = swap(ready, XY, 1), swap(ready, XY, 2)
    *kv_parts, aside, across = lax.optimization_barrier((*kv_parts, aside, across))

    kv, dkv, probs, dscores = attend(
        mine, kv_parts, queries, out_grad, image_ids, text_sample
    )
    cut = projected.shape[0] // 2
    upper, lower, _ = lax.optimization_barrier((across[:cut], aside[cut:], dkv))
    upper, lower = swap(upper, XY, 1), swap(lower, XY, 2)
    dkv_own = [dkv] + [swap(dkv, T, 2 * k) for k in range(1, chips)]
    turned = turn(after(feats, dkv))
    attended, d_queries = finish(kv, probs, dscores)
    stacked = lax.optimization_barrier((*dkv_own, turned, attended, d_queries, upper, lower))
    *dkv_own, turned, attended, d_queries, upper, lower = stacked
    dkv_other = swap(pack(*dkv_own), T, 1)

    back_out = back(dkv_own, dkv_other, kv_weight, parts)
    d_rows, sent, columns = back_out[0], back_out[1:-2], back_out[-2]
    sent = [swap(x, XY, j + 1) for j, x in enumerate(sent)]
    early = parts // 2
    partial, bias = first_grad(turned, [d_rows] + sent[: early - 1])
    d_weight, d_bias = last_grad(turned, partial, bias, sent[early - 1 :])
    ours = lax.optimization_barrier((columns, *sent, bias))[:-1]
    theirs = swap(pack(*ours), T, 1)
    d_kv_weight = kv_grad(
        (projected, aside, across, upper, lower), columns, sent, theirs
    )
    return attended, d_queries, d_weight, d_bias.reshape(-1), d_kv_weight


def solution(mesh):
    in_specs = (
        P("tensor", ("group", "dp")),
        P(("group", "dp"), "tensor"),
        P("tensor"),
        P("tensor", None),
        P(("group", "dp"), "tensor"),
        P(("group", "dp"), "tensor"),
        P(("group", "dp"), None),
        P(("group", "dp"), None),
    )
    out_specs = (
        P(("group", "dp"), "tensor"),
        P(("group", "dp"), "tensor"),
        P(("group", "dp"), "tensor"),
        P("tensor"),
        P("tensor", ("group", "dp")),
    )
    return jax.shard_map(shards, mesh=mesh, in_specs=in_specs, out_specs=out_specs, check_vma=False)
```
